32 devices in a mesh: space: 4 (over y, x), blk: 8 (over z, core).
Axes of the slice: x: 2, y: 2, z: 4, core: 2. Of those that a mesh axis runs over, the one named last changes fastest.
Arguments:
- snapshots: bfloat16 [32, 512, 3, 2048], P('blk', None, None, 'space'), may hold values from -6 to 6
- quadrature: float32 [2048], P('space'), may hold values from 0.2 to 5
- omega: float32 [16, 2, 32, 16], replicated, may hold values from -6 to 6
Outputs:
- modes: float32 [16, 2, 16, 3, 2048], P('blk', None, None, None, 'space')
- energies: float32 [16, 16], replicated
The draws below stay inside these ranges and needn't reach their ends.
All inputs are finite; a program needn't handle non-finite values.
Results may differ from the reference program's by a relative error of at most 0.0051.
Values may be sent and summed in bfloat16 or wider, within the bound.
No kernel may reach another device: no remote copies, remote signals or barrier semaphores. Data moves between devices by JAX's collectives and lax.ppermute only.
A program may use at most 64 MiB of HBM per device.

```python
import math
import jax
import jax.numpy as jnp
from jax import lax

NT = 512
NF = 16
RANK = 16
COMP = 3
ITERS = 2
NS_STEPS = 14
POINTS = 2048
DOFS = 6144
BLOCKS = 32


def shard_levels(key, shape, split, least, high):
    loudness, own = 1.0, jax.random.fold_in(key, 6)
    for dim, blocks in split:
        steps = jnp.exp(jax.random.uniform(jax.random.fold_in(own, dim), (blocks,), jnp.float32, least / len(split), high / len(split)))
        loudness = loudness * jnp.repeat(steps, shape[dim] // blocks).reshape([-1 if axis == dim else 1 for axis in range(len(shape))])
    return loudness


def centred(rng, shape, width, limit, cuts=(), kind=jnp.bfloat16):
    array = jax.random.normal(rng, shape, jnp.float32) * width
    if len(cuts) > 0:
        array = shard_levels(rng, shape, cuts, -0.22, 0.18) * array
    return jnp.clip(array, min=-limit, max=limit).astype(kind)


def setup_inputs(seed: int = 0) -> dict:
    keys = jax.random.split(jax.random.key(seed), 4)
    snapshots = centred(keys[0], (BLOCKS, NT, COMP, POINTS), 1.0, 6.0, ((0, 8), (3, 4)))
    quadrature = jnp.clip(jnp.exp(math.log(5.0) - 3.218876 * jax.random.uniform(keys[1], (POINTS,), jnp.float32) ** shard_levels(keys[1], (POINTS,), ((0, 4),), -0.2, 0.2)), 0.2, 5.0)
    omega = centred(keys[2], (NF, 2, BLOCKS, RANK), 1.0, 6.0, (), jnp.float32)
    return dict(snapshots=snapshots, quadrature=quadrature, omega=omega)


def dft_table(sample_count, harmonic_count):
    sample = jnp.arange(sample_count, dtype=jnp.int32)
    harmonic = jnp.arange(1, harmonic_count + 1, dtype=jnp.int32)
    phase_turns = harmonic[:, None] * sample[None, :] % sample_count
    phases = 2.0 * math.pi / sample_count * phase_turns.astype(jnp.float32)
    ramp_angle = 2.0 * math.pi / sample_count * sample.astype(jnp.float32)
    window = 0.5 - 0.5 * jnp.cos(ramp_angle)
    factor = 1.0 / jnp.sqrt(jnp.sum(window * window))
    real_part = window * jnp.cos(phases) * factor
    imag_part = -window * jnp.sin(phases) * factor
    return jnp.concatenate([real_part, imag_part], 0).astype(jnp.bfloat16)

def batch_mm(left_mat, right_mat):
    return jnp.einsum('fab,fbc->fac', left_mat, right_mat, precision=lax.Precision.HIGHEST)

def cplx_mul(left_re, left_im, right_re, right_im):
    return (batch_mm(left_re, right_re) - batch_mm(left_im, right_im), batch_mm(left_re, right_im) + batch_mm(left_im, right_re))

def herm_mul(left_re, left_im, right_re, right_im):
    tl_re = jnp.swapaxes(left_re, 1, 2)
    tl_im = jnp.swapaxes(left_im, 1, 2)
    return (batch_mm(tl_re, right_re) + batch_mm(tl_im, right_im), batch_mm(tl_re, right_im) - batch_mm(tl_im, right_re))

def inverse_root(gram_re, gram_im):
    rank_count = gram_re.shape[-1]
    upper_half = jnp.concatenate([gram_re, -gram_im], -1)
    lower_half = jnp.concatenate([gram_im, gram_re], -1)
    joined = jnp.concatenate([upper_half, lower_half], -2)
    frob_norm = jnp.sqrt(lax.optimization_barrier(jnp.sum(joined * joined, axis=(1, 2))))[:, None, None]
    identity_mat = jnp.eye(2 * rank_count, dtype=jnp.float32)
    root_state = joined / frob_norm
    inverse_state = jnp.broadcast_to(identity_mat, joined.shape)
    for repeat_index in range(NS_STEPS):
        factor = 1.5 * identity_mat - 0.5 * batch_mm(inverse_state, root_state)
        root_state = batch_mm(root_state, factor)
        inverse_state = batch_mm(factor, inverse_state)
    inverse_state = inverse_state / jnp.sqrt(frob_norm)
    return (inverse_state[:, :rank_count, :rank_count], inverse_state[:, rank_count:, :rank_count])

def subspace(gram_re, gram_im, coef_re, coef_im):
    for repeat_index in range(ITERS):
        next_re, next_im = cplx_mul(gram_re, gram_im, coef_re, coef_im)
        image_re, image_im = cplx_mul(gram_re, gram_im, next_re, next_im)
        inner_re, inner_im = herm_mul(next_re, next_im, image_re, image_im)
        root_re, root_im = inverse_root(inner_re, inner_im)
        coef_re, coef_im = cplx_mul(next_re, next_im, root_re, root_im)
    final_re, final_im = cplx_mul(gram_re, gram_im, coef_re, coef_im)
    energies = lax.optimization_barrier(jnp.sum(final_re * final_re + final_im * final_im, axis=1))
    return (coef_re, coef_im, energies)

def reference(snapshots, quadrature, omega):
    kernel = dft_table(NT, NF)
    flattened = snapshots.reshape(BLOCKS, NT, DOFS)

    def one_block(one_snap):
        return jnp.dot(kernel, one_snap, preferred_element_type=jnp.float32)
    spectra = lax.map(one_block, flattened)
    root_weight = jnp.tile(jnp.sqrt(quadrature), COMP)
    weighted = (spectra * root_weight).astype(jnp.bfloat16)
    by_freq = jnp.transpose(weighted.reshape(BLOCKS, 2, NF, DOFS), (2, 1, 0, 3))

    def one_gram(freq_pair):
        re_rows = freq_pair[0]
        im_rows = freq_pair[1]
        rr_sum = jnp.dot(re_rows, re_rows.T, preferred_element_type=jnp.float32)
        ii_sum = jnp.dot(im_rows, im_rows.T, preferred_element_type=jnp.float32)
        ri_sum = jnp.dot(re_rows, im_rows.T, preferred_element_type=jnp.float32)
        ir_sum = jnp.dot(im_rows, re_rows.T, preferred_element_type=jnp.float32)
        return jnp.stack([rr_sum + ii_sum, ri_sum - ir_sum], 0)
    gram_matrix = lax.map(one_gram, by_freq) / DOFS
    coef_re, coef_im, energies = subspace(gram_matrix[:, 0], gram_matrix[:, 1], omega[:, 0], omega[:, 1])
    coef_low = jnp.stack([coef_re, coef_im], 1).astype(jnp.bfloat16)

    def one_mode(item_pair):
        freq_pair, coef_pair = item_pair
        re_rows = freq_pair[0]
        im_rows = freq_pair[1]
        coef_real = coef_pair[0].T
        coef_imag = coef_pair[1].T
        out_re = jnp.dot(coef_real, re_rows, preferred_element_type=jnp.float32) - jnp.dot(coef_imag, im_rows, preferred_element_type=jnp.float32)
        out_im = jnp.dot(coef_imag, re_rows, preferred_element_type=jnp.float32) + jnp.dot(coef_real, im_rows, preferred_element_type=jnp.float32)
        return jnp.stack([out_re, out_im], 0)
    modes = lax.map(one_mode, (by_freq, coef_low)) * (1.0 / root_weight)
    return (modes.reshape(NF, 2, RANK, COMP, POINTS), energies)
```

```python
import functools
import math

import jax
import jax.numpy as jnp
import ml_dtypes
import numpy as np
from jax import lax
from jax.experimental import pallas as pl
from jax.experimental.pallas import tpu as pltpu
from jax.sharding import PartitionSpec as P

NF = 16
RANK = 16
ITERS = 2
NS_STEPS = 14
IN_FLIGHT = 6
LIMIT = 40 * 2**20
F32, BF16 = jnp.float32, jnp.bfloat16
HBM = pl.BlockSpec(memory_space=pltpu.HBM)
VMEM = pl.BlockSpec(memory_space=pltpu.VMEM)


def in_hbm(array):
    return pltpu.with_memory_space_constraint(array, pltpu.HBM)


def dft_table(sample_count, harmonic_count):
    sample = np.arange(sample_count, dtype=np.int32)
    harmonic = np.arange(1, harmonic_count + 1, dtype=np.int32)
    turns = harmonic[:, None] * sample[None, :] % sample_count
    phases = np.float32(2.0 * math.pi / sample_count) * turns.astype(np.float32)
    window = np.float32(0.5) - np.float32(0.5) * np.cos(
        np.float32(2.0 * math.pi / sample_count) * sample.astype(np.float32)
    )
    factor = np.float32(1.0) / np.sqrt(np.sum(window * window, dtype=np.float32))
    return np.stack([window * np.cos(phases) * factor, -window * np.sin(phases) * factor])


def wide_table(sample_count, groups, blocks):
    share = NF // groups
    rows = dft_table(sample_count, NF).reshape(2, groups, share, sample_count).transpose(1, 0, 2, 3)
    wide = np.zeros((groups, 2, share, blocks, blocks, sample_count), np.float32)
    for block in range(blocks):
        wide[:, :, :, block, block] = rows
    return wide.reshape(2 * NF * blocks, blocks * sample_count).astype(ml_dtypes.bfloat16)


def iota(shape, axis):
    return lax.broadcasted_iota(jnp.int32, shape, axis)


def mm(left, right, contract=(1, 0)):
    dims = (((contract[0],), (contract[1],)), ((), ()))
    return lax.dot_general(
        left, right, dims, precision=lax.Precision.HIGHEST, preferred_element_type=F32
    )


def spectra_kernel(groups, snap, table_hbm, quad_hbm, *refs):
    outs, (buf, table, quad, piles, sems, small) = refs[:-6], refs[-6:]
    blocks, comps, samples, points = snap.shape
    steps = [(c, b) for c in range(comps) for b in range(blocks)]
    copies = [
        pltpu.make_async_copy(snap.at[b, c], buf.at[b, c], sems.at[i])
        for i, (c, b) in enumerate(steps)
    ]
    table_copy = pltpu.make_async_copy(table_hbm, table, small.at[0])
    quad_copy = pltpu.make_async_copy(quad_hbm, quad, small.at[1])
    table_copy.start()
    quad_copy.start()
    for copy in copies[:IN_FLIGHT]:
        copy.start()
    me = lax.axis_index("blk")
    table_copy.wait()
    quad_copy.wait()
    root = jnp.sqrt(quad[...])
    height = piles.shape[1]
    for i, (c, b) in enumerate(steps):
        copies[i].wait()
        if i + IN_FLIGHT < len(copies):
            copies[i + IN_FLIGHT].start()
        part = jnp.dot(
            table[:, b * samples : (b + 1) * samples], buf[b, c], preferred_element_type=F32
        )
        total = part if b == 0 else total + part
        if b == blocks - 1:
            low = (total * root).astype(BF16)
            for owner in range(groups):
                piles[owner, :, c * points : (c + 1) * points] = low[
                    owner * height : (owner + 1) * height
                ]
    for far, out in enumerate(outs):
        for core in range(2):
            out[core] = piles[me ^ (2 * far + core)]


def start_kernel(share, blocks, omega, _, out, own, sem):
    me = lax.axis_index("blk")
    copy = pltpu.make_async_copy(omega.at[pl.ds(me * share, share)], own, sem)
    copy.start()
    copy.wait()
    total = own.shape[-1]
    half = share * blocks
    rows = 2 * share * total
    row, col = iota((rows, total), 0), iota((rows, total), 1)
    source, part, freq, block = row // (2 * half), row // half % 2, row // blocks % share, row % blocks
    hit = (source ^ me) * blocks + block == col
    columns = []
    for f in range(share):
        real, imag = own[f, 0], own[f, 1]
        for first, second in ((real, imag), (-imag, real)):
            upper = jnp.where(hit & (freq == f) & (part == 0), 1.0, 0.0)
            lower = jnp.where(hit & (freq == f) & (part == 1), 1.0, 0.0)
            columns.append(mm(upper, first, (1, 1)) + mm(lower, second, (1, 1)))
    for i, column in enumerate(columns):
        out[:, i * RANK : (i + 1) * RANK] = column


def swap_lanes(value, half):
    width = value.shape[-1]
    axis = value.ndim - 1
    lane = iota(value.shape, axis)
    down = pltpu.roll(value, half, axis)
    up = pltpu.roll(value, width - half, axis)
    return jnp.where(lane // half % 2 == 0, up, down)


def stacked(refs):
    if refs[0].shape[0] % 16 == 0:
        return jnp.concatenate([ref[...] for ref in refs], 0)
    return jnp.concatenate([ref[...].astype(F32) for ref in refs], 0).astype(BF16)


def gram_kernel(share, blocks, *refs):
    pieces, out = refs[:-1], refs[-1]
    half = share * blocks
    data = stacked(pieces)
    size = data.shape[0]
    products = lax.dot_general(data, data, (((1,), (1,)), ((), ())), preferred_element_type=F32)
    if half != 8:
        row, lane = iota((size, size), 0), iota((size, size), 1)
        turned = swap_lanes(products, half)
        down, up = pltpu.roll(turned, half, 0), pltpu.roll(turned, size - half, 0)
        same = (row // half + lane // half) % 2 == 0
        out[...] = jnp.where(same, products, -products) + jnp.where(row // half % 2 == 0, up, down)
        return
    sources = size // 16
    products = products.reshape(sources, 2, 8, size)
    shape = (sources, 8, size)
    row, lane = iota(shape, 1), iota(shape, 2)
    real = products[:, 0]
    value = jnp.where(lane // half % 2 == 0, real, -real) + swap_lanes(products[:, 1], half)
    value = jnp.where(row // blocks == lane // blocks % share, value, 0.0)
    if share == 2:
        value = (value + pltpu.roll(value, 4, 1)).reshape(sources // 2, 2, 8, size)
        value = jnp.where(iota((sources // 2, 8, size), 1) < 4, value[:, 0], value[:, 1])
    out[...] = value.reshape(out.shape)


def spread_gram(value, share, blocks):
    half = share * blocks
    size = value.shape[-1]
    if half != 8:
        row, lane = iota((size, size), 0), iota((size, size), 1)
        return jnp.where(row // blocks % share == lane // blocks % share, value, 0.0)
    sources = size // 16
    shape = (sources, 8, size)
    row, lane = iota(shape, 1), iota(shape, 2)
    if share == 2:
        value = value.reshape(sources // 2, 8, size)
        other = pltpu.roll(value, 4, 1)
        low = iota(value.shape, 1) < 4
        value = jnp.stack([jnp.where(low, value, other), jnp.where(low, other, value)], 1)
    value = value.reshape(shape)
    value = jnp.where(row // blocks == lane // blocks % share, value, 0.0)
    turned = swap_lanes(value, half)
    turned = jnp.where(lane // half % 2 == 0, -turned, turned)
    return jnp.stack([value, turned], 1).reshape(size, size)


def inverse_root(inner, share):
    size = inner.shape[0]
    width = size // share
    identity = jnp.where(iota((size, size), 0) == iota((size, size), 1), 1.0, 0.0)
    norms = []
    for f in range(share):
        block = inner[f * width : (f + 1) * width]
        norms.append(jnp.broadcast_to(jnp.sqrt(jnp.sum(block * block, keepdims=True)), block.shape))
    norm = norms[0] if share == 1 else jnp.concatenate(norms, 0)
    joint = inner / norm
    inverse = None
    for step in range(NS_STEPS):
        factor = 1.5 * identity - 0.5 * joint
        if step < NS_STEPS - 1:
            joint = mm(mm(joint, factor), factor)
        inverse = factor if step == 0 else mm(factor, inverse)
    return inverse / jnp.sqrt(norm)


def subspace_kernel(share, blocks, dofs, grams, *refs):
    parts, (start, coef_out, energy_out) = refs[:grams], refs[grams:]
    value = parts[0][...]
    for part in parts[1:]:
        value = value + part[...]
    gram = spread_gram(value * (1.0 / dofs), share, blocks)
    nxt = mm(gram, start[...])
    for step in range(ITERS):
        image = mm(gram, nxt)
        root = inverse_root(mm(nxt, image, (0, 0)), share)
        if step < ITERS - 1:
            nxt = mm(image, root)
    coef, image = mm(nxt, root), mm(image, root)
    half = share * blocks
    row, lane = iota(coef.shape, 0), iota(coef.shape, 1)
    same = (row // half + lane // RANK) % 2 == 0
    coef_out[...] = jnp.where(same, coef, -coef).astype(BF16)
    energy = jnp.sum(image * image, axis=0, keepdims=True)
    me = lax.axis_index("blk")
    energy_out[...] = jnp.zeros_like(energy_out)
    for f in range(share):
        energy_out[pl.ds(me * share + f, 1), :] = energy[:, 2 * f * RANK : (2 * f + 1) * RANK]


def modes_kernel(share, quad, coef, *refs):
    pieces, out = refs[:-1], refs[-1]
    data = stacked(pieces)
    points = quad.shape[-1]
    inverse = 1.0 / jnp.sqrt(quad[...])
    for c in range(data.shape[-1] // points):
        modes = lax.dot_general(
            coef[...],
            data[:, c * points : (c + 1) * points],
            (((0,), (0,)), ((), ())),
            preferred_element_type=F32,
        )
        modes = modes * inverse
        for f in range(share):
            for part in range(2):
                at = (2 * f + part) * RANK
                out[f, part, c] = modes[at : at + RANK]


def call(kernel, outs, specs, name, scratch=()):
    return pl.pallas_call(
        kernel,
        out_shape=outs,
        in_specs=specs,
        out_specs=jax.tree.map(lambda _: VMEM, outs),
        scratch_shapes=list(scratch),
        compiler_params=pltpu.CompilerParams(vmem_limit_bytes=LIMIT),
        name=name,
    )


def exchange(array, axis, distance):
    size = lax.axis_size(axis)
    return lax.ppermute(array, axis, [(i, i ^ distance) for i in range(size)])


def per_device(snapshots, quadrature, omega):
    blocks, samples, comps, points = snapshots.shape
    groups, spaces = lax.axis_size("blk"), lax.axis_size("space")
    share = NF // groups
    reach = groups // 2
    height = 2 * share * blocks
    width = comps * points
    size = groups * height
    piece = (height, width)

    table = in_hbm(jnp.asarray(wide_table(samples, groups, blocks)))
    quad = quadrature.reshape(1, points)
    steps = blocks * comps
    spectra = call(
        functools.partial(spectra_kernel, groups),
        [jax.ShapeDtypeStruct((2, *piece), BF16)] * reach,
        [HBM] * 3,
        "spectra",
        [
            pltpu.VMEM((blocks, comps, samples, points), BF16),
            pltpu.VMEM(table.shape, BF16),
            pltpu.VMEM((1, points), F32),
            pltpu.VMEM((groups, *piece), BF16),
            pltpu.SemaphoreType.DMA((steps,)),
            pltpu.SemaphoreType.DMA((2,)),
        ],
    )(in_hbm(snapshots.transpose(0, 2, 1, 3)), table, in_hbm(quad))

    start = call(
        functools.partial(start_kernel, share, blocks),
        jax.ShapeDtypeStruct((size, 2 * share * RANK), F32),
        [HBM, pl.BlockSpec(memory_space=pl.ANY)],
        "start",
        [pltpu.VMEM((share, 2, RANK, groups * blocks), F32), pltpu.SemaphoreType.DMA],
    )(in_hbm(omega.transpose(0, 1, 3, 2)), spectra[0])

    pieces = [None] * groups
    pieces[0] = spectra[0][0]
    arrived = {far: exchange(spectra[far], "blk", 2 * far) for far in range(reach - 1, 0, -1)}
    pieces[1] = exchange(spectra[0][1], "blk", 1)
    for far in range(reach - 1, 0, -1):
        pieces[2 * far] = arrived[far][0]
        pieces[2 * far + 1] = exchange(arrived[far][1], "blk", 1)

    packed = (size * (blocks if share * blocks == 8 else height) // height, size)
    gram = call(
        functools.partial(gram_kernel, share, blocks),
        jax.ShapeDtypeStruct(packed, F32),
        [VMEM] * groups,
        "gram",
    )(*pieces)
    if spaces <= 4:
        grams = [gram] + [exchange(gram, "space", d) for d in range(spaces - 1, 0, -1)]
    else:
        grams = [lax.psum(gram, "space")]

    coef, energies = call(
        functools.partial(subspace_kernel, share, blocks, width * spaces, len(grams)),
        [
            jax.ShapeDtypeStruct((size, 2 * share * RANK), BF16),
            jax.ShapeDtypeStruct((NF, RANK), F32),
        ],
        [VMEM] * (len(grams) + 1),
        "subspace",
    )(*grams, start)

    modes = call(
        functools.partial(modes_kernel, share),
        jax.ShapeDtypeStruct((share, 2, comps, RANK, points), F32),
        [VMEM] * (groups + 2),
        "modes",
    )(quad, coef, *pieces)

    energies = energies + exchange(energies, "blk", 1)
    shares = [exchange(energies, "blk", 2 * far) for far in range(reach - 1, 0, -1)]
    for other in shares:
        energies = energies + other
    return modes.transpose(0, 1, 3, 2, 4), energies


def solution(mesh):
    in_specs = (P("blk", None, None, "space"), P("space"), P())
    out_specs = (P("blk", None, None, None, "space"), P())
    return jax.shard_map(
        per_device, mesh=mesh, in_specs=in_specs, out_specs=out_specs, check_vma=False
    )
```

```python
import functools
import math

import jax
import jax.numpy as jnp
import ml_dtypes
import numpy as np
from jax import lax
from jax.experimental import pallas as pl
from jax.experimental.pallas import tpu as pltpu
from jax.sharding import PartitionSpec as P

NF = 16
RANK = 16
ITERS = 2
NS_STEPS = 14
FULL_STEPS = 6
WIDTH = 2 * RANK
COPIES = 4
IN_FLIGHT = 6
LIMIT = 40 * 2**20
F32, BF16 = jnp.float32, jnp.bfloat16
HBM = pl.BlockSpec(memory_space=pltpu.HBM)
VMEM = pl.BlockSpec(memory_space=pltpu.VMEM)


def in_hbm(array):
    return pltpu.with_memory_space_constraint(array, pltpu.HBM)


def dft_table(sample_count, harmonic_count):
    sample = np.arange(sample_count, dtype=np.int32)
    harmonic = np.arange(1, harmonic_count + 1, dtype=np.int32)
    turns = harmonic[:, None] * sample[None, :] % sample_count
    phases = np.float32(2.0 * math.pi / sample_count) * turns.astype(np.float32)
    window = np.float32(0.5) - np.float32(0.5) * np.cos(
        np.float32(2.0 * math.pi / sample_count) * sample.astype(np.float32)
    )
    factor = np.float32(1.0) / np.sqrt(np.sum(window * window, dtype=np.float32))
    return np.stack([window * np.cos(phases) * factor, -window * np.sin(phases) * factor])


def wide_table(sample_count, groups, blocks):
    share = NF // groups
    rows = dft_table(sample_count, NF).reshape(2, groups, share, sample_count).transpose(1, 0, 2, 3)
    wide = np.zeros((groups, 2, share, blocks, blocks, sample_count), np.float32)
    for block in range(blocks):
        wide[:, :, :, block, block] = rows
    return wide.reshape(2 * NF * blocks, blocks * sample_count).astype(ml_dtypes.bfloat16)


def iota(shape, axis):
    return lax.broadcasted_iota(jnp.int32, shape, axis)


def mm(left, right, contract=(1, 0)):
    dims = (((contract[0],), (contract[1],)), ((), ()))
    return lax.dot_general(
        left, right, dims, precision=lax.Precision.HIGHEST, preferred_element_type=F32
    )


def spectra_kernel(groups, snap, table_hbm, quad_hbm, *refs):
    outs, (buf, table, quad, piles, sems, small) = refs[:-6], refs[-6:]
    blocks, comps, samples, points = snap.shape
    steps = [(c, b) for c in range(comps) for b in range(blocks)]
    copies = [
        pltpu.make_async_copy(snap.at[b, c], buf.at[b, c], sems.at[i])
        for i, (c, b) in enumerate(steps)
    ]
    table_copy = pltpu.make_async_copy(table_hbm, table, small.at[0])
    quad_copy = pltpu.make_async_copy(quad_hbm, quad, small.at[1])
    table_copy.start()
    quad_copy.start()
    for copy in copies[:IN_FLIGHT]:
        copy.start()
    me = lax.axis_index("blk")
    table_copy.wait()
    quad_copy.wait()
    root = jnp.sqrt(quad[...])
    height = piles.shape[1]
    for i, (c, b) in enumerate(steps):
        copies[i].wait()
        if i + IN_FLIGHT < len(copies):
            copies[i + IN_FLIGHT].start()
        part = jnp.dot(
            table[:, b * samples : (b + 1) * samples], buf[b, c], preferred_element_type=F32
        )
        total = part if b == 0 else total + part
        if b == blocks - 1:
            low = (total * root).astype(BF16)
            for owner in range(groups):
                piles[owner, :, c * points : (c + 1) * points] = low[
                    owner * height : (owner + 1) * height
                ]
    for far, out in enumerate(outs):
        for core in range(2):
            out[core] = piles[me ^ (2 * far + core)]


def start_kernel(share, blocks, omega, _, wide_out, tall_out, own, sem):
    me = lax.axis_index("blk")
    copy = pltpu.make_async_copy(omega.at[pl.ds(me * share, share)], own, sem)
    copy.start()
    copy.wait()
    total = own.shape[-1]
    half = share * blocks
    size = 2 * share * total

    def placed(shape, axis, f, part):
        index, block = iota(shape, axis), iota(shape, 1 - axis)
        same = ((index // (2 * half)) ^ me) * blocks + index % blocks == block
        return jnp.where(same & (index // blocks % share == f) & (index // half % 2 == part), 1.0, 0.0)

    for f in range(share):
        real, imag = own[f, 0], own[f, 1]
        first = jnp.concatenate([real, -imag], 0)
        second = jnp.concatenate([imag, real], 0)
        wide_out[f] = mm(
            placed((size, total), 0, f, 0), jnp.concatenate([first] * COPIES, 0), (1, 1)
        ) + mm(placed((size, total), 0, f, 1), jnp.concatenate([second] * COPIES, 0), (1, 1))
        tall_out[f * WIDTH : (f + 1) * WIDTH] = mm(
            first, placed((total, size), 1, f, 0)
        ) + mm(second, placed((total, size), 1, f, 1))


def swap_lanes(value, half):
    width = value.shape[-1]
    axis = value.ndim - 1
    lane = iota(value.shape, axis)
    down = pltpu.roll(value, half, axis)
    up = pltpu.roll(value, width - half, axis)
    return jnp.where(lane // half % 2 == 0, up, down)


def stacked(refs):
    if refs[0].shape[0] % 16 == 0:
        return jnp.concatenate([ref[...] for ref in refs], 0)
    return jnp.concatenate([ref[...].astype(F32) for ref in refs], 0).astype(BF16)


def gram_kernel(share, blocks, *refs):
    pieces, out = refs[:-1], refs[-1]
    half = share * blocks
    data = stacked(pieces)
    size = data.shape[0]
    products = lax.dot_general(data, data, (((1,), (1,)), ((), ())), preferred_element_type=F32)
    if half != 8:
        row, lane = iota((size, size), 0), iota((size, size), 1)
        turned = swap_lanes(products, half)
        down, up = pltpu.roll(turned, half, 0), pltpu.roll(turned, size - half, 0)
        same = (row // half + lane // half) % 2 == 0
        out[...] = jnp.where(same, products, -products) + jnp.where(row // half % 2 == 0, up, down)
        return
    sources = size // 16
    products = products.reshape(sources, 2, 8, size)
    shape = (sources, 8, size)
    row, lane = iota(shape, 1), iota(shape, 2)
    real = products[:, 0]
    value = jnp.where(lane // half % 2 == 0, real, -real) + swap_lanes(products[:, 1], half)
    value = jnp.where(row // blocks == lane // blocks % share, value, 0.0)
    if share == 2:
        value = (value + pltpu.roll(value, 4, 1)).reshape(sources // 2, 2, 8, size)
        value = jnp.where(iota((sources // 2, 8, size), 1) < 4, value[:, 0], value[:, 1])
    out[...] = value.reshape(out.shape)


def spread_gram(value, share, blocks):
    half = share * blocks
    size = value.shape[-1]
    if half != 8:
        row, lane = iota((size, size), 0), iota((size, size), 1)
        return jnp.where(row // blocks % share == lane // blocks % share, value, 0.0)
    sources = size // 16
    shape = (sources, 8, size)
    row, lane = iota(shape, 1), iota(shape, 2)
    if share == 2:
        value = value.reshape(sources // 2, 8, size)
        other = pltpu.roll(value, 4, 1)
        low = iota(value.shape, 1) < 4
        value = jnp.stack([jnp.where(low, value, other), jnp.where(low, other, value)], 1)
    value = value.reshape(shape)
    value = jnp.where(row // blocks == lane // blocks % share, value, 0.0)
    turned = swap_lanes(value, half)
    turned = jnp.where(lane // half % 2 == 0, -turned, turned)
    return jnp.stack([value, turned], 1).reshape(size, size)


def thirds(value):
    high = value.astype(BF16)
    rest = value - high.astype(F32)
    middle = rest.astype(BF16)
    return high, middle, (rest - middle.astype(F32)).astype(BF16)


def packed_mm(left, right, full=True):
    high, middle, low = thirds(left)
    group = iota(left.shape, 1) // WIDTH
    first = jnp.where(group == 2, middle, high)
    top, mid, end = right
    total = jnp.dot(first, jnp.concatenate([top, mid, top, end], 0), preferred_element_type=F32)
    if full:
        second = jnp.where(group == 0, middle, low)[:, : 2 * WIDTH]
        total = total + jnp.dot(second, jnp.concatenate([mid, top], 0), preferred_element_type=F32)
    return total


def inverse_roots(inners):
    shape = inners[0].shape
    identity = jnp.where(iota(shape, 0) == iota(shape, 1) % WIDTH, 1.0, 0.0)
    norms = [
        jnp.sqrt(jnp.sum(inner * inner, keepdims=True) * (1.0 / COPIES)) for inner in inners
    ]
    rests = [identity - inner / norm for inner, norm in zip(inners, norms)]
    roots = [identity + 0.5 * rest for rest in rests]
    for step in range(1, NS_STEPS):
        full = step <= FULL_STEPS
        rights = [thirds(rest) for rest in rests]
        squares = [packed_mm(e, r, full) for e, r in zip(rests, rights)]
        cubes = [packed_mm(s, r, full) for s, r in zip(squares, rights)]
        if step > 1:
            roots = [z + 0.5 * packed_mm(z, r, full) for z, r in zip(roots, rights)]
        rests = [0.75 * s + 0.25 * c for s, c in zip(squares, cubes)]
    rights = [thirds(rest) for rest in rests]
    roots = [z + 0.5 * packed_mm(z, r, False) for z, r in zip(roots, rights)]
    return [z * (1.0 / jnp.sqrt(norm)) for z, norm in zip(roots, norms)]


def subspace_kernel(share, blocks, dofs, grams, *refs):
    parts, (wide, tall, coef_out, energy_out) = refs[:grams], refs[grams:]
    value = parts[0][...]
    for part in parts[1:]:
        value = value + part[...]
    gram = spread_gram(value * (1.0 / dofs), share, blocks)
    freqs = range(share)
    tall_next = mm(tall[...], gram)
    images = [mm(gram, mm(gram, wide[f])) for f in freqs]
    for step in range(ITERS):
        rows = [tall_next[f * WIDTH : (f + 1) * WIDTH] for f in freqs]
        inners = [mm(rows[f], images[f]) for f in freqs]
        if step < ITERS - 1:
            tall_image = mm(tall_next, gram)
            ahead = [mm(gram, image) for image in images]
        roots = inverse_roots(inners)
        rights = [thirds(root) for root in roots]
        if step < ITERS - 1:
            tall_next = jnp.concatenate(
                [
                    packed_mm(roots[f], thirds(tall_image[f * WIDTH : (f + 1) * WIDTH]))
                    for f in freqs
                ],
                0,
            )
            images = [packed_mm(ahead[f], rights[f]) for f in freqs]
    half = share * blocks
    me = lax.axis_index("blk")
    energy_out[...] = jnp.zeros_like(energy_out)
    for f in freqs:
        final = packed_mm(images[f], rights[f])
        energy = jnp.sum(final * final, axis=0, keepdims=True)
        energy_out[pl.ds(me * share + f, 1), :] = energy[:, :RANK]
    for f in freqs:
        coef = packed_mm(roots[f], thirds(rows[f]))
        same = (iota(coef.shape, 0) // RANK + iota(coef.shape, 1) // half) % 2 == 0
        coef_out[f * WIDTH : (f + 1) * WIDTH] = jnp.where(same, coef, -coef).astype(BF16)


def modes_kernel(share, quad, coef, *refs):
    pieces, out = refs[:-1], refs[-1]
    data = stacked(pieces)
    points = quad.shape[-1]
    inverse = 1.0 / jnp.sqrt(quad[...])
    for c in range(data.shape[-1] // points):
        modes = inverse * jnp.dot(
            coef[...], data[:, c * points : (c + 1) * points], preferred_element_type=F32
        )
        for f in range(share):
            for part in range(2):
                at = (2 * f + part) * RANK
                out[f, part, c] = modes[at : at + RANK]


def call(kernel, outs, specs, name, scratch=()):
    return pl.pallas_call(
        kernel,
        out_shape=outs,
        in_specs=specs,
        out_specs=jax.tree.map(lambda _: VMEM, outs),
        scratch_shapes=list(scratch),
        compiler_params=pltpu.CompilerParams(vmem_limit_bytes=LIMIT),
        name=name,
    )


def exchange(array, axis, distance):
    size = lax.axis_size(axis)
    return lax.ppermute(array, axis, [(i, i ^ distance) for i in range(size)])


def per_device(snapshots, quadrature, omega):
    blocks, samples, comps, points = snapshots.shape
    groups, spaces = lax.axis_size("blk"), lax.axis_size("space")
    share = NF // groups
    reach = groups // 2
    height = 2 * share * blocks
    width = comps * points
    size = groups * height
    piece = (height, width)

    table = in_hbm(jnp.asarray(wide_table(samples, groups, blocks)))
    quad = quadrature.reshape(1, points)
    steps = blocks * comps
    spectra = call(
        functools.partial(spectra_kernel, groups),
        [jax.ShapeDtypeStruct((2, *piece), BF16)] * reach,
        [HBM] * 3,
        "spectra",
        [
            pltpu.VMEM((blocks, comps, samples, points), BF16),
            pltpu.VMEM(table.shape, BF16),
            pltpu.VMEM((1, points), F32),
            pltpu.VMEM((groups, *piece), BF16),
            pltpu.SemaphoreType.DMA((steps,)),
            pltpu.SemaphoreType.DMA((2,)),
        ],
    )(in_hbm(snapshots.transpose(0, 2, 1, 3)), table, in_hbm(quad))

    wide, tall = call(
        functools.partial(start_kernel, share, blocks),
        [
            jax.ShapeDtypeStruct((share, size, COPIES * WIDTH), F32),
            jax.ShapeDtypeStruct((share * WIDTH, size), F32),
        ],
        [HBM, pl.BlockSpec(memory_space=pl.ANY)],
        "start",
        [pltpu.VMEM((share, 2, RANK, groups * blocks), F32), pltpu.SemaphoreType.DMA],
    )(in_hbm(omega.transpose(0, 1, 3, 2)), spectra[0])

    pieces = [None] * groups
    pieces[0] = spectra[0][0]
    arrived = {far: exchange(spectra[far], "blk", 2 * far) for far in range(reach - 1, 0, -1)}
    pieces[1] = exchange(spectra[0][1], "blk", 1)
    wide, tall, arrived[1] = lax.optimization_barrier((wide, tall, arrived[1]))
    for far in range(reach - 1, 0, -1):
        pieces[2 * far] = arrived[far][0]
        pieces[2 * far + 1] = exchange(arrived[far][1], "blk", 1)

    packed = (size * (blocks if share * blocks == 8 else height) // height, size)
    gram = call(
        functools.partial(gram_kernel, share, blocks),
        jax.ShapeDtypeStruct(packed, F32),
        [VMEM] * groups,
        "gram",
    )(*pieces)
    if spaces <= 4:
        grams = [gram] + [exchange(gram, "space", d) for d in range(1, spaces)]
    else:
        grams = [lax.psum(gram, "space")]

    coef, energies = call(
        functools.partial(subspace_kernel, share, blocks, width * spaces, len(grams)),
        [
            jax.ShapeDtypeStruct((share * WIDTH, size), BF16),
            jax.ShapeDtypeStruct((NF, RANK), F32),
        ],
        [VMEM] * (len(grams) + 2),
        "subspace",
    )(*grams, wide, tall)

    modes = call(
        functools.partial(modes_kernel, share),
        jax.ShapeDtypeStruct((share, 2, comps, RANK, points), F32),
        [VMEM] * (groups + 2),
        "modes",
    )(quad, coef, *pieces)

    energies = energies + exchange(energies, "blk", 1)
    shares = [exchange(energies, "blk", 2 * far) for far in range(1, reach)]
    for other in shares:
        energies = energies + other
    return modes.transpose(0, 1, 3, 2, 4), energies


def solution(mesh):
    in_specs = (P("blk", None, None, "space"), P("space"), P())
    out_specs = (P("blk", None, None, None, "space"), P())
    return jax.shard_map(
        per_device, mesh=mesh, in_specs=in_specs, out_specs=out_specs, check_vma=False
    )
```

```python
import functools
import math

import jax
import jax.numpy as jnp
import ml_dtypes
import numpy as np
from jax import lax
from jax.experimental import pallas as pl
from jax.experimental.pallas import tpu as pltpu
from jax.sharding import PartitionSpec as P

NF = 16
RANK = 16
ITERS = 2
NS_STEPS = 14
FULL_STEPS = 6
WIDTH = 2 * RANK
COPIES = 4
IN_FLIGHT = 8
LIMIT = 40 * 2**20
F32, BF16 = jnp.float32, jnp.bfloat16
HBM = pl.BlockSpec(memory_space=pltpu.HBM)
VMEM = pl.BlockSpec(memory_space=pltpu.VMEM)


def in_hbm(array):
    return pltpu.with_memory_space_constraint(array, pltpu.HBM)


def dft_table(sample_count, harmonic_count):
    sample = np.arange(sample_count, dtype=np.int32)
    harmonic = np.arange(1, harmonic_count + 1, dtype=np.int32)
    turns = harmonic[:, None] * sample[None, :] % sample_count
    phases = np.float32(2.0 * math.pi / sample_count) * turns.astype(np.float32)
    window = np.float32(0.5) - np.float32(0.5) * np.cos(
        np.float32(2.0 * math.pi / sample_count) * sample.astype(np.float32)
    )
    factor = np.float32(1.0) / np.sqrt(np.sum(window * window, dtype=np.float32))
    return np.stack([window * np.cos(phases) * factor, -window * np.sin(phases) * factor])


def wide_table(sample_count, groups, blocks):
    share = NF // groups
    rows = dft_table(sample_count, NF).reshape(2, groups, share, sample_count).transpose(1, 0, 2, 3)
    wide = np.zeros((groups, 2, share, blocks, blocks, sample_count), np.float32)
    for block in range(blocks):
        wide[:, :, :, block, block] = rows
    return wide.reshape(2 * NF * blocks, blocks * sample_count).astype(ml_dtypes.bfloat16)


def iota(shape, axis):
    return lax.broadcasted_iota(jnp.int32, shape, axis)


def mm(left, right, contract=(1, 0)):
    dims = (((contract[0],), (contract[1],)), ((), ()))
    return lax.dot_general(
        left, right, dims, precision=lax.Precision.HIGHEST, preferred_element_type=F32
    )


def spectra_kernel(groups, snap, table_hbm, quad_hbm, *refs):
    outs, (buf, table, quad, piles, sems, small) = refs[:-6], refs[-6:]
    blocks, comps, samples, points = snap.shape
    steps = [(c, b) for c in range(comps) for b in range(blocks)]
    copies = [
        pltpu.make_async_copy(snap.at[b, c], buf.at[b, c], sems.at[i])
        for i, (c, b) in enumerate(steps)
    ]
    table_copy = pltpu.make_async_copy(table_hbm, table, small.at[0])
    quad_copy = pltpu.make_async_copy(quad_hbm, quad, small.at[1])
    table_copy.start()
    quad_copy.start()
    for copy in copies[:IN_FLIGHT]:
        copy.start()
    me = lax.axis_index("blk")
    table_copy.wait()
    quad_copy.wait()
    root = jnp.sqrt(quad[...])
    height = piles.shape[1]
    for i, (c, b) in enumerate(steps):
        copies[i].wait()
        if i + IN_FLIGHT < len(copies):
            copies[i + IN_FLIGHT].start()
        part = jnp.dot(
            table[:, b * samples : (b + 1) * samples], buf[b, c], preferred_element_type=F32
        )
        total = part if b == 0 else total + part
        if b == blocks - 1:
            low = (total * root).astype(BF16)
            for owner in range(groups):
                piles[owner, :, c * points : (c + 1) * points] = low[
                    owner * height : (owner + 1) * height
                ]
    for far, out in enumerate(outs):
        for core in range(2):
            out[core] = piles[me ^ (2 * far + core)]


def start_kernel(share, blocks, omega, _, wide_out, tall_out, own, sem):
    me = lax.axis_index("blk")
    copy = pltpu.make_async_copy(omega.at[pl.ds(me * share, share)], own, sem)
    copy.start()
    copy.wait()
    total = own.shape[-1]
    half = share * blocks
    size = 2 * share * total

    def placed(shape, axis, f, part):
        index, block = iota(shape, axis), iota(shape, 1 - axis)
        same = ((index // (2 * half)) ^ me) * blocks + index % blocks == block
        return jnp.where(same & (index // blocks % share == f) & (index // half % 2 == part), 1.0, 0.0)

    for f in range(share):
        real, imag = own[f, 0], own[f, 1]
        first = jnp.concatenate([real, -imag], 0)
        second = jnp.concatenate([imag, real], 0)
        wide_out[f] = mm(
            placed((size, total), 0, f, 0), jnp.concatenate([first] * COPIES, 0), (1, 1)
        ) + mm(placed((size, total), 0, f, 1), jnp.concatenate([second] * COPIES, 0), (1, 1))
        tall_out[f * WIDTH : (f + 1) * WIDTH] = mm(
            first, placed((total, size), 1, f, 0)
        ) + mm(second, placed((total, size), 1, f, 1))


def swap_lanes(value, half):
    width = value.shape[-1]
    axis = value.ndim - 1
    lane = iota(value.shape, axis)
    down = pltpu.roll(value, half, axis)
    up = pltpu.roll(value, width - half, axis)
    return jnp.where(lane // half % 2 == 0, up, down)


def stacked(refs):
    if refs[0].shape[0] % 16 == 0:
        return jnp.concatenate([ref[...] for ref in refs], 0)
    return jnp.concatenate([ref[...].astype(F32) for ref in refs], 0).astype(BF16)


def gram_kernel(share, blocks, *refs):
    pieces, out = refs[:-1], refs[-1]
    half = share * blocks
    data = stacked(pieces)
    size = data.shape[0]
    products = lax.dot_general(data, data, (((1,), (1,)), ((), ())), preferred_element_type=F32)
    if half != 8:
        row, lane = iota((size, size), 0), iota((size, size), 1)
        turned = swap_lanes(products, half)
        down, up = pltpu.roll(turned, half, 0), pltpu.roll(turned, size - half, 0)
        same = (row // half + lane // half) % 2 == 0
        out[...] = jnp.where(same, products, -products) + jnp.where(row // half % 2 == 0, up, down)
        return
    sources = size // 16
    products = products.reshape(sources, 2, 8, size)
    shape = (sources, 8, size)
    row, lane = iota(shape, 1), iota(shape, 2)
    real = products[:, 0]
    value = jnp.where(lane // half % 2 == 0, real, -real) + swap_lanes(products[:, 1], half)
    value = jnp.where(row // blocks == lane // blocks % share, value, 0.0)
    if share == 2:
        value = (value + pltpu.roll(value, 4, 1)).reshape(sources // 2, 2, 8, size)
        value = jnp.where(iota((sources // 2, 8, size), 1) < 4, value[:, 0], value[:, 1])
    out[...] = value.reshape(out.shape)


def spread_gram(value, share, blocks):
    half = share * blocks
    size = value.shape[-1]
    if half != 8:
        row, lane = iota((size, size), 0), iota((size, size), 1)
        return jnp.where(row // blocks % share == lane // blocks % share, value, 0.0)
    sources = size // 16
    shape = (sources, 8, size)
    row, lane = iota(shape, 1), iota(shape, 2)
    if share == 2:
        value = value.reshape(sources // 2, 8, size)
        other = pltpu.roll(value, 4, 1)
        low = iota(value.shape, 1) < 4
        value = jnp.stack([jnp.where(low, value, other), jnp.where(low, other, value)], 1)
    value = value.reshape(shape)
    value = jnp.where(row // blocks == lane // blocks % share, value, 0.0)
    turned = swap_lanes(value, half)
    turned = jnp.where(lane // half % 2 == 0, -turned, turned)
    return jnp.stack([value, turned], 1).reshape(size, size)


def thirds(value):
    high = value.astype(BF16)
    rest = value - high.astype(F32)
    middle = rest.astype(BF16)
    return high, middle, (rest - middle.astype(F32)).astype(BF16)


def packed_mm(left, right, full=True):
    high, middle, low = thirds(left)
    group = iota(left.shape, 1) // WIDTH
    first = jnp.where(group == 2, middle, high)
    top, mid, end = right
    total = jnp.dot(first, jnp.concatenate([top, mid, top, end], 0), preferred_element_type=F32)
    if full:
        second = jnp.where(group == 0, middle, low)[:, : 2 * WIDTH]
        total = total + jnp.dot(second, jnp.concatenate([mid, top], 0), preferred_element_type=F32)
    return total


def inverse_roots(inners):
    shape = inners[0].shape
    identity = jnp.where(iota(shape, 0) == iota(shape, 1) % WIDTH, 1.0, 0.0)
    norms = [
        jnp.sqrt(jnp.sum(inner * inner, keepdims=True) * (1.0 / COPIES)) for inner in inners
    ]
    rests = [identity - inner / norm for inner, norm in zip(inners, norms)]
    roots = [identity + 0.5 * rest for rest in rests]
    for step in range(1, NS_STEPS):
        full = step <= FULL_STEPS
        rights = [thirds(rest) for rest in rests]
        squares = [packed_mm(e, r, full) for e, r in zip(rests, rights)]
        cubes = [packed_mm(s, r, full) for s, r in zip(squares, rights)]
        if step > 1:
            roots = [z + 0.5 * packed_mm(z, r, full) for z, r in zip(roots, rights)]
        rests = [0.75 * s + 0.25 * c for s, c in zip(squares, cubes)]
    rights = [thirds(rest) for rest in rests]
    roots = [z + 0.5 * packed_mm(z, r, False) for z, r in zip(roots, rights)]
    return [z * (1.0 / jnp.sqrt(norm)) for z, norm in zip(roots, norms)]


def subspace_kernel(share, blocks, dofs, grams, *refs):
    parts, (wide, tall, coef_out, energy_out) = refs[:grams], refs[grams:]
    value = parts[0][...]
    for part in parts[1:]:
        value = value + part[...]
    gram = spread_gram(value * (1.0 / dofs), share, blocks)
    freqs = range(share)
    tall_next = mm(tall[...], gram)
    images = [mm(gram, mm(gram, wide[f])) for f in freqs]
    for step in range(ITERS):
        rows = [tall_next[f * WIDTH : (f + 1) * WIDTH] for f in freqs]
        inners = [mm(rows[f], images[f]) for f in freqs]
        if step < ITERS - 1:
            tall_image = mm(tall_next, gram)
            ahead = [mm(gram, image) for image in images]
        roots = inverse_roots(inners)
        rights = [thirds(root) for root in roots]
        if step < ITERS - 1:
            tall_next = jnp.concatenate(
                [
                    packed_mm(roots[f], thirds(tall_image[f * WIDTH : (f + 1) * WIDTH]))
                    for f in freqs
                ],
                0,
            )
            images = [packed_mm(ahead[f], rights[f]) for f in freqs]
    half = share * blocks
    me = lax.axis_index("blk")
    energy_out[...] = jnp.zeros_like(energy_out)
    for f in freqs:
        final = packed_mm(images[f], rights[f])
        energy = jnp.sum(final * final, axis=0, keepdims=True)
        energy_out[pl.ds(me * share + f, 1), :] = energy[:, :RANK]
    for f in freqs:
        coef = packed_mm(roots[f], thirds(rows[f]))
        same = (iota(coef.shape, 0) // RANK + iota(coef.shape, 1) // half) % 2 == 0
        coef_out[f * WIDTH : (f + 1) * WIDTH] = jnp.where(same, coef, -coef).astype(BF16)


def modes_kernel(share, quad, coef, *refs):
    pieces, out = refs[:-1], refs[-1]
    data = stacked(pieces)
    points = quad.shape[-1]
    inverse = 1.0 / jnp.sqrt(quad[...])
    for c in range(data.shape[-1] // points):
        modes = inverse * jnp.dot(
            coef[...], data[:, c * points : (c + 1) * points], preferred_element_type=F32
        )
        for f in range(share):
            for part in range(2):
                at = (2 * f + part) * RANK
                out[f, part, c] = modes[at : at + RANK]


def call(kernel, outs, specs, name, scratch=()):
    return pl.pallas_call(
        kernel,
        out_shape=outs,
        in_specs=specs,
        out_specs=jax.tree.map(lambda _: VMEM, outs),
        scratch_shapes=list(scratch),
        compiler_params=pltpu.CompilerParams(vmem_limit_bytes=LIMIT),
        name=name,
    )


def exchange(array, axis, distance):
    size = lax.axis_size(axis)
    return lax.ppermute(array, axis, [(i, i ^ distance) for i in range(size)])


def per_device(snapshots, quadrature, omega):
    blocks, samples, comps, points = snapshots.shape
    groups, spaces = lax.axis_size("blk"), lax.axis_size("space")
    share = NF // groups
    reach = groups // 2
    height = 2 * share * blocks
    width = comps * points
    size = groups * height
    piece = (height, width)

    table = in_hbm(jnp.asarray(wide_table(samples, groups, blocks)))
    quad = quadrature.reshape(1, points)
    steps = blocks * comps
    spectra = call(
        functools.partial(spectra_kernel, groups),
        [jax.ShapeDtypeStruct((2, *piece), BF16)] * reach,
        [HBM] * 3,
        "spectra",
        [
            pltpu.VMEM((blocks, comps, samples, points), BF16),
            pltpu.VMEM(table.shape, BF16),
            pltpu.VMEM((1, points), F32),
            pltpu.VMEM((groups, *piece), BF16),
            pltpu.SemaphoreType.DMA((steps,)),
            pltpu.SemaphoreType.DMA((2,)),
        ],
    )(in_hbm(snapshots.transpose(0, 2, 1, 3)), table, in_hbm(quad))

    wide, tall = call(
        functools.partial(start_kernel, share, blocks),
        [
            jax.ShapeDtypeStruct((share, size, COPIES * WIDTH), F32),
            jax.ShapeDtypeStruct((share * WIDTH, size), F32),
        ],
        [HBM, pl.BlockSpec(memory_space=pl.ANY)],
        "start",
        [pltpu.VMEM((share, 2, RANK, groups * blocks), F32), pltpu.SemaphoreType.DMA],
    )(in_hbm(omega.transpose(0, 1, 3, 2)), spectra[0])

    arrived = {far: exchange(spectra[far], "blk", 2 * far) for far in range(reach - 1, 0, -1)}
    wide, tall, arrived = lax.optimization_barrier((wide, tall, arrived))
    arrived[0] = spectra[0]
    sent = exchange(jnp.stack([arrived[far][1] for far in range(reach)]), "blk", 1)
    pieces = [piece for far in range(reach) for piece in (arrived[far][0], sent[far])]

    packed = (size * (blocks if share * blocks == 8 else height) // height, size)
    gram = call(
        functools.partial(gram_kernel, share, blocks),
        jax.ShapeDtypeStruct(packed, F32),
        [VMEM] * groups,
        "gram",
    )(*pieces)
    if spaces <= 4:
        grams = [gram] + [exchange(gram, "space", d) for d in range(1, spaces)]
    else:
        grams = [lax.psum(gram, "space")]

    coef, energies = call(
        functools.partial(subspace_kernel, share, blocks, width * spaces, len(grams)),
        [
            jax.ShapeDtypeStruct((share * WIDTH, size), BF16),
            jax.ShapeDtypeStruct((NF, RANK), F32),
        ],
        [VMEM] * (len(grams) + 2),
        "subspace",
    )(*grams, wide, tall)

    modes = call(
        functools.partial(modes_kernel, share),
        jax.ShapeDtypeStruct((share, 2, comps, RANK, points), F32),
        [VMEM] * (groups + 2),
        "modes",
    )(quad, coef, *pieces)

    energies = energies + exchange(energies, "blk", 1)
    shares = [exchange(energies, "blk", 2 * far) for far in range(1, reach)]
    for other in shares:
        energies = energies + other
    return modes.transpose(0, 1, 3, 2, 4), energies


def solution(mesh):
    in_specs = (P("blk", None, None, "space"), P("space"), P())
    out_specs = (P("blk", None, None, None, "space"), P())
    return jax.shard_map(
        per_device, mesh=mesh, in_specs=in_specs, out_specs=out_specs, check_vma=False
    )
```

```python
import functools
import math

import jax
import jax.numpy as jnp
import ml_dtypes
import numpy as np
from jax import lax
from jax.experimental import pallas as pl
from jax.experimental.pallas import tpu as pltpu
from jax.sharding import PartitionSpec as P

NF = 16
RANK = 16
ITERS = 2
NS_STEPS = 14
FULL_STEPS = 6
WIDTH = 2 * RANK
COPIES = 4
IN_FLIGHT = 8
LIMIT = 40 * 2**20
F32, BF16 = jnp.float32, jnp.bfloat16
HBM = pl.BlockSpec(memory_space=pltpu.HBM)
VMEM = pl.BlockSpec(memory_space=pltpu.VMEM)


def in_hbm(array):
    return pltpu.with_memory_space_constraint(array, pltpu.HBM)


def dft_table(sample_count, harmonic_count):
    sample = np.arange(sample_count, dtype=np.int32)
    harmonic = np.arange(1, harmonic_count + 1, dtype=np.int32)
    turns = harmonic[:, None] * sample[None, :] % sample_count
    phases = np.float32(2.0 * math.pi / sample_count) * turns.astype(np.float32)
    window = np.float32(0.5) - np.float32(0.5) * np.cos(
        np.float32(2.0 * math.pi / sample_count) * sample.astype(np.float32)
    )
    factor = np.float32(1.0) / np.sqrt(np.sum(window * window, dtype=np.float32))
    return np.stack([window * np.cos(phases) * factor, -window * np.sin(phases) * factor])


def table_rows(sample_count, groups):
    rows = dft_table(sample_count, NF).reshape(2, groups, NF // groups, sample_count)
    rows = rows.transpose(1, 0, 2, 3).reshape(2 * NF, sample_count)
    return rows.astype(ml_dtypes.bfloat16)


def iota(shape, axis):
    return lax.broadcasted_iota(jnp.int32, shape, axis)


def mm(left, right, contract=(1, 0)):
    dims = (((contract[0],), (contract[1],)), ((), ()))
    return lax.dot_general(
        left, right, dims, precision=lax.Precision.HIGHEST, preferred_element_type=F32
    )


def spectra_kernel(groups, snap, table_hbm, quad_hbm, *refs):
    outs, (buf, thin, quad, table, piles, sems, small) = refs[:-7], refs[-7:]
    blocks, comps, samples, points = snap.shape
    steps = [(c, b) for c in range(comps) for b in range(blocks)]
    copies = [
        pltpu.make_async_copy(snap.at[b, c], buf.at[b, c], sems.at[i])
        for i, (c, b) in enumerate(steps)
    ]
    table_copy = pltpu.make_async_copy(table_hbm, thin, small.at[0])
    quad_copy = pltpu.make_async_copy(quad_hbm, quad, small.at[1])
    table_copy.start()
    quad_copy.start()
    for copy in copies[:IN_FLIGHT]:
        copy.start()
    me = lax.axis_index("blk")
    height = piles.shape[1]
    table_copy.wait()
    shape = (table.shape[0], thin.shape[0])
    spread = jnp.where(iota(shape, 0) // blocks == iota(shape, 1), 1.0, 0.0).astype(BF16)
    spread = jnp.dot(spread, thin[...], preferred_element_type=F32)
    for b in range(blocks):
        table[:, b * samples : (b + 1) * samples] = jnp.where(
            iota(spread.shape, 0) % blocks == b, spread, 0.0
        ).astype(BF16)
    quad_copy.wait()
    root = jnp.sqrt(quad[...])
    for i, (c, b) in enumerate(steps):
        copies[i].wait()
        if i + IN_FLIGHT < len(copies):
            copies[i + IN_FLIGHT].start()
        part = jnp.dot(
            table[:, b * samples : (b + 1) * samples], buf[b, c], preferred_element_type=F32
        )
        total = part if b == 0 else total + part
        if b == blocks - 1:
            low = (total * root).astype(BF16)
            for owner in range(groups):
                piles[owner, :, c * points : (c + 1) * points] = low[
                    owner * height : (owner + 1) * height
                ]
    for far, out in enumerate(outs):
        for core in range(2):
            out[core] = piles[me ^ (2 * far + core)]


def start_kernel(share, blocks, omega, _, wide_out, tall_out, own, sem):
    me = lax.axis_index("blk")
    copy = pltpu.make_async_copy(omega.at[pl.ds(me * share, share)], own, sem)
    copy.start()
    copy.wait()
    total = own.shape[-1]
    half = share * blocks
    size = 2 * share * total

    def placed(shape, axis, f, part):
        index, block = iota(shape, axis), iota(shape, 1 - axis)
        same = ((index // (2 * half)) ^ me) * blocks + index % blocks == block
        return jnp.where(same & (index // blocks % share == f) & (index // half % 2 == part), 1.0, 0.0)

    for f in range(share):
        real, imag = own[f, 0], own[f, 1]
        first = jnp.concatenate([real, -imag], 0)
        second = jnp.concatenate([imag, real], 0)
        wide_out[f] = mm(
            placed((size, total), 0, f, 0), jnp.concatenate([first] * COPIES, 0), (1, 1)
        ) + mm(placed((size, total), 0, f, 1), jnp.concatenate([second] * COPIES, 0), (1, 1))
        tall_out[f * WIDTH : (f + 1) * WIDTH] = mm(
            first, placed((total, size), 1, f, 0)
        ) + mm(second, placed((total, size), 1, f, 1))


def swap_lanes(value, half):
    width = value.shape[-1]
    axis = value.ndim - 1
    lane = iota(value.shape, axis)
    down = pltpu.roll(value, half, axis)
    up = pltpu.roll(value, width - half, axis)
    return jnp.where(lane // half % 2 == 0, up, down)


def stacked(refs):
    if refs[0].shape[0] % 16 == 0:
        return jnp.concatenate([ref[...] for ref in refs], 0)
    return jnp.concatenate([ref[...].astype(F32) for ref in refs], 0).astype(BF16)


def gram_kernel(share, blocks, *refs):
    pieces, out = refs[:-1], refs[-1]
    half = share * blocks
    data = stacked(pieces)
    size = data.shape[0]
    products = lax.dot_general(data, data, (((1,), (1,)), ((), ())), preferred_element_type=F32)
    if half != 8:
        row, lane = iota((size, size), 0), iota((size, size), 1)
        turned = swap_lanes(products, half)
        down, up = pltpu.roll(turned, half, 0), pltpu.roll(turned, size - half, 0)
        same = (row // half + lane // half) % 2 == 0
        out[...] = jnp.where(same, products, -products) + jnp.where(row // half % 2 == 0, up, down)
        return
    sources = size // 16
    products = products.reshape(sources, 2, 8, size)
    shape = (sources, 8, size)
    row, lane = iota(shape, 1), iota(shape, 2)
    real = products[:, 0]
    value = jnp.where(lane // half % 2 == 0, real, -real) + swap_lanes(products[:, 1], half)
    value = jnp.where(row // blocks == lane // blocks % share, value, 0.0)
    if share == 2:
        value = (value + pltpu.roll(value, 4, 1)).reshape(sources // 2, 2, 8, size)
        value = jnp.where(iota((sources // 2, 8, size), 1) < 4, value[:, 0], value[:, 1])
    out[...] = value.reshape(out.shape)


def spread_gram(value, share, blocks):
    half = share * blocks
    size = value.shape[-1]
    if half != 8:
        row, lane = iota((size, size), 0), iota((size, size), 1)
        return jnp.where(row // blocks % share == lane // blocks % share, value, 0.0)
    sources = size // 16
    shape = (sources, 8, size)
    row, lane = iota(shape, 1), iota(shape, 2)
    if share == 2:
        value = value.reshape(sources // 2, 8, size)
        other = pltpu.roll(value, 4, 1)
        low = iota(value.shape, 1) < 4
        value = jnp.stack([jnp.where(low, value, other), jnp.where(low, other, value)], 1)
    value = value.reshape(shape)
    value = jnp.where(row // blocks == lane // blocks % share, value, 0.0)
    turned = swap_lanes(value, half)
    turned = jnp.where(lane // half % 2 == 0, -turned, turned)
    return jnp.stack([value, turned], 1).reshape(size, size)


def thirds(value):
    high = value.astype(BF16)
    rest = value - high.astype(F32)
    middle = rest.astype(BF16)
    return high, middle, (rest - middle.astype(F32)).astype(BF16)


def packed_mm(left, right, full=True):
    high, middle, low = thirds(left)
    top, mid, end = right
    group = iota(left.shape, 1) // WIDTH
    terms = [top, mid, top, end]
    lanes = jnp.where(group == 2, middle, high)
    if full:
        terms += [mid, top]
        rest = jnp.where(group == 0, middle, low)[:, : 2 * WIDTH]
        lanes = jnp.concatenate([lanes, rest], 1)
    return jnp.dot(lanes, jnp.concatenate(terms, 0), preferred_element_type=F32)


def inverse_roots(inners, lefts, rights):
    shape = inners[0].shape
    identity = jnp.where(iota(shape, 0) == iota(shape, 1) % WIDTH, 1.0, 0.0)
    squares = [packed_mm(inner, thirds(inner)) for inner in inners]
    norms = [
        jnp.sqrt(jnp.sum(inner * inner, keepdims=True) * (1.0 / COPIES)) for inner in inners
    ]
    scales = [1.0 / norm for norm in norms]
    rests = [identity - inner * scale for inner, scale in zip(inners, scales)]
    squares = [
        2.0 * rest - identity + square * scale * scale
        for rest, square, scale in zip(rests, squares, scales)
    ]
    roots = None
    for step in range(NS_STEPS - 1):
        full = step < FULL_STEPS
        terms = [thirds(rest) for rest in rests]
        if step > 0:
            squares = [packed_mm(e, r, full) for e, r in zip(rests, terms)]
            roots = [z + 0.5 * packed_mm(z, r, full) for z, r in zip(roots, terms)]
        else:
            roots = [identity + 0.5 * e for e in rests]
        cubes = [packed_mm(s, r, full) for s, r in zip(squares, terms)]
        rests = [0.75 * s + 0.25 * c for s, c in zip(squares, cubes)]
    scales = [1.0 / jnp.sqrt(norm) for norm in norms]
    lefts = [packed_mm(z, thirds(left)) for z, left in zip(roots, lefts)]
    rights = [packed_mm(right, thirds(z)) for z, right in zip(roots, rights)]
    lefts = [
        (left + 0.5 * packed_mm(e, thirds(left), False)) * scale
        for e, left, scale in zip(rests, lefts, scales)
    ]
    rights = [
        (right + 0.5 * packed_mm(right, thirds(e), False)) * scale
        for e, right, scale in zip(rests, rights, scales)
    ]
    return lefts, rights


def subspace_kernel(share, blocks, dofs, grams, *refs):
    parts, (wide, tall, coef_out, energy_out) = refs[:grams], refs[grams:]
    value = parts[0][...]
    for part in parts[1:]:
        value = value + part[...]
    gram = spread_gram(value * (1.0 / dofs), share, blocks)
    freqs = range(share)
    tall_next = mm(tall[...], gram)
    images = [mm(gram, mm(gram, wide[f])) for f in freqs]
    rows = [tall_next[f * WIDTH : (f + 1) * WIDTH] for f in freqs]
    for _ in range(ITERS - 1):
        inners = [mm(rows[f], images[f]) for f in freqs]
        tall_image = mm(jnp.concatenate(rows, 0), gram)
        ahead = [mm(gram, image) for image in images]
        rows = [tall_image[f * WIDTH : (f + 1) * WIDTH] for f in freqs]
        rows, images = inverse_roots(inners, rows, ahead)
    inners = [mm(rows[f], images[f]) for f in freqs]
    coefs, finals = inverse_roots(inners, rows, images)
    half = share * blocks
    me = lax.axis_index("blk")
    energy_out[...] = jnp.zeros_like(energy_out)
    for f, (coef, final) in enumerate(zip(coefs, finals)):
        energy = jnp.sum(final * final, axis=0, keepdims=True)
        energy_out[pl.ds(me * share + f, 1), :] = energy[:, :RANK]
        same = (iota(coef.shape, 0) // RANK + iota(coef.shape, 1) // half) % 2 == 0
        coef_out[f * WIDTH : (f + 1) * WIDTH] = jnp.where(same, coef, -coef).astype(BF16)


def modes_kernel(share, quad, coef, *refs):
    pieces, out = refs[:-1], refs[-1]
    data = stacked(pieces)
    points = quad.shape[-1]
    inverse = 1.0 / jnp.sqrt(quad[...])
    for c in range(data.shape[-1] // points):
        modes = inverse * jnp.dot(
            coef[...], data[:, c * points : (c + 1) * points], preferred_element_type=F32
        )
        for f in range(share):
            for part in range(2):
                at = (2 * f + part) * RANK
                out[f, part, c] = modes[at : at + RANK]


def call(kernel, outs, specs, name, scratch=()):
    return pl.pallas_call(
        kernel,
        out_shape=outs,
        in_specs=specs,
        out_specs=jax.tree.map(lambda _: VMEM, outs),
        scratch_shapes=list(scratch),
        compiler_params=pltpu.CompilerParams(vmem_limit_bytes=LIMIT),
        name=name,
    )


def exchange(array, axis, distance):
    size = lax.axis_size(axis)
    return lax.ppermute(array, axis, [(i, i ^ distance) for i in range(size)])


def per_device(snapshots, quadrature, omega):
    blocks, samples, comps, points = snapshots.shape
    groups, spaces = lax.axis_size("blk"), lax.axis_size("space")
    share = NF // groups
    reach = groups // 2
    height = 2 * share * blocks
    width = comps * points
    size = groups * height
    piece = (height, width)

    table = in_hbm(jnp.asarray(table_rows(samples, groups)))
    quad = quadrature.reshape(1, points)
    steps = blocks * comps
    spectra = call(
        functools.partial(spectra_kernel, groups),
        [jax.ShapeDtypeStruct((2, *piece), BF16)] * reach,
        [HBM] * 3,
        "spectra",
        [
            pltpu.VMEM((blocks, comps, samples, points), BF16),
            pltpu.VMEM(table.shape, BF16),
            pltpu.VMEM((1, points), F32),
            pltpu.VMEM((size, blocks * samples), BF16),
            pltpu.VMEM((groups, *piece), BF16),
            pltpu.SemaphoreType.DMA((steps,)),
            pltpu.SemaphoreType.DMA((2,)),
        ],
    )(in_hbm(snapshots.transpose(0, 2, 1, 3)), table, in_hbm(quad))

    wide, tall = call(
        functools.partial(start_kernel, share, blocks),
        [
            jax.ShapeDtypeStruct((share, size, COPIES * WIDTH), F32),
            jax.ShapeDtypeStruct((share * WIDTH, size), F32),
        ],
        [HBM, pl.BlockSpec(memory_space=pl.ANY)],
        "start",
        [pltpu.VMEM((share, 2, RANK, groups * blocks), F32), pltpu.SemaphoreType.DMA],
    )(in_hbm(omega.transpose(0, 1, 3, 2)), spectra[0])

    arrived = {far: exchange(spectra[far], "blk", 2 * far) for far in range(reach - 1, 0, -1)}
    wide, tall, arrived = lax.optimization_barrier((wide, tall, arrived))
    arrived[0] = spectra[0]
    sent = exchange(jnp.stack([arrived[far][1] for far in range(reach)]), "blk", 1)
    pieces = [piece for far in range(reach) for piece in (arrived[far][0], sent[far])]

    packed = (size * (blocks if share * blocks == 8 else height) // height, size)
    gram = call(
        functools.partial(gram_kernel, share, blocks),
        jax.ShapeDtypeStruct(packed, F32),
        [VMEM] * groups,
        "gram",
    )(*pieces)
    if spaces <= 4:
        grams = [gram] + [exchange(gram, "space", d) for d in range(1, spaces)]
    else:
        grams = [lax.psum(gram, "space")]

    coef, energies = call(
        functools.partial(subspace_kernel, share, blocks, width * spaces, len(grams)),
        [
            jax.ShapeDtypeStruct((share * WIDTH, size), BF16),
            jax.ShapeDtypeStruct((NF, RANK), F32),
        ],
        [VMEM] * (len(grams) + 2),
        "subspace",
    )(*grams, wide, tall)

    modes = call(
        functools.partial(modes_kernel, share),
        jax.ShapeDtypeStruct((share, 2, comps, RANK, points), F32),
        [VMEM] * (groups + 2),
        "modes",
    )(quad, coef, *pieces)

    energies = energies + exchange(energies, "blk", 1)
    shares = [exchange(energies, "blk", 2 * far) for far in range(1, reach)]
    for other in shares:
        energies = energies + other
    return modes.transpose(0, 1, 3, 2, 4), energies


def solution(mesh):
    in_specs = (P("blk", None, None, "space"), P("space"), P())
    out_specs = (P("blk", None, None, None, "space"), P())
    return jax.shard_map(
        per_device, mesh=mesh, in_specs=in_specs, out_specs=out_specs, check_vma=False
    )
```

```python
import functools
import math

import jax
import jax.numpy as jnp
import ml_dtypes
import numpy as np
from jax import lax
from jax.experimental import pallas as pl
from jax.experimental.pallas import tpu as pltpu
from jax.sharding import PartitionSpec as P

NF = 16
RANK = 16
ITERS = 2
NS_STEPS = 14
FULL_STEPS = 6
WIDTH = 2 * RANK
COPIES = 4
IN_FLIGHT = 8
LIMIT = 40 * 2**20
F32, BF16 = jnp.float32, jnp.bfloat16
HBM = pl.BlockSpec(memory_space=pltpu.HBM)
VMEM = pl.BlockSpec(memory_space=pltpu.VMEM)


def in_hbm(array):
    return pltpu.with_memory_space_constraint(array, pltpu.HBM)


def dft_table(sample_count, harmonic_count):
    sample = np.arange(sample_count, dtype=np.int32)
    harmonic = np.arange(1, harmonic_count + 1, dtype=np.int32)
    turns = harmonic[:, None] * sample[None, :] % sample_count
    phases = np.float32(2.0 * math.pi / sample_count) * turns.astype(np.float32)
    window = np.float32(0.5) - np.float32(0.5) * np.cos(
        np.float32(2.0 * math.pi / sample_count) * sample.astype(np.float32)
    )
    factor = np.float32(1.0) / np.sqrt(np.sum(window * window, dtype=np.float32))
    return np.stack([window * np.cos(phases) * factor, -window * np.sin(phases) * factor])


def table_rows(sample_count, groups):
    rows = dft_table(sample_count, NF).reshape(2, groups, NF // groups, sample_count)
    rows = rows.transpose(1, 0, 2, 3).reshape(2 * NF, sample_count)
    return rows.astype(ml_dtypes.bfloat16)


def iota(shape, axis):
    return lax.broadcasted_iota(jnp.int32, shape, axis)


def mm(left, right, contract=(1, 0)):
    dims = (((contract[0],), (contract[1],)), ((), ()))
    return lax.dot_general(
        left, right, dims, precision=lax.Precision.HIGHEST, preferred_element_type=F32
    )


def spectra_kernel(groups, snap, table_hbm, quad_hbm, *refs):
    outs, (buf, thin, quad, table, piles, sems, small) = refs[:-7], refs[-7:]
    blocks, comps, samples, points = snap.shape
    steps = [(c, b) for c in range(comps) for b in range(blocks)]
    copies = [
        pltpu.make_async_copy(snap.at[b, c], buf.at[b, c], sems.at[i])
        for i, (c, b) in enumerate(steps)
    ]
    table_copy = pltpu.make_async_copy(table_hbm, thin, small.at[0])
    quad_copy = pltpu.make_async_copy(quad_hbm, quad, small.at[1])
    table_copy.start()
    quad_copy.start()
    for copy in copies[:IN_FLIGHT]:
        copy.start()
    me = lax.axis_index("blk")
    height = piles.shape[1]
    table_copy.wait()
    shape = (table.shape[0], thin.shape[0])
    spread = jnp.where(iota(shape, 0) // blocks == iota(shape, 1), 1.0, 0.0).astype(BF16)
    spread = jnp.dot(spread, thin[...], preferred_element_type=F32)
    for b in range(blocks):
        table[:, b * samples : (b + 1) * samples] = jnp.where(
            iota(spread.shape, 0) % blocks == b, spread, 0.0
        ).astype(BF16)
    quad_copy.wait()
    root = jnp.sqrt(quad[...])
    for i, (c, b) in enumerate(steps):
        copies[i].wait()
        if i + IN_FLIGHT < len(copies):
            copies[i + IN_FLIGHT].start()
        part = jnp.dot(
            table[:, b * samples : (b + 1) * samples], buf[b, c], preferred_element_type=F32
        )
        total = part if b == 0 else total + part
        if b == blocks - 1:
            low = (total * root).astype(BF16)
            for owner in range(groups):
                piles[owner, :, c * points : (c + 1) * points] = low[
                    owner * height : (owner + 1) * height
                ]
    for far, out in enumerate(outs):
        for core in range(2):
            out[core] = piles[me ^ (2 * far + core)]


def start_kernel(share, blocks, omega, _, wide_out, tall_out, own, sem):
    me = lax.axis_index("blk")
    copy = pltpu.make_async_copy(omega.at[pl.ds(me * share, share)], own, sem)
    copy.start()
    copy.wait()
    total = own.shape[-1]
    half = share * blocks
    size = 2 * share * total

    def placed(shape, axis, f, part):
        index, block = iota(shape, axis), iota(shape, 1 - axis)
        same = ((index // (2 * half)) ^ me) * blocks + index % blocks == block
        return jnp.where(same & (index // blocks % share == f) & (index // half % 2 == part), 1.0, 0.0)

    for f in range(share):
        real, imag = own[f, 0], own[f, 1]
        first = jnp.concatenate([real, -imag], 0)
        second = jnp.concatenate([imag, real], 0)
        wide_out[f] = mm(
            placed((size, total), 0, f, 0), jnp.concatenate([first] * COPIES, 0), (1, 1)
        ) + mm(placed((size, total), 0, f, 1), jnp.concatenate([second] * COPIES, 0), (1, 1))
        tall_out[f * WIDTH : (f + 1) * WIDTH] = mm(
            first, placed((total, size), 1, f, 0)
        ) + mm(second, placed((total, size), 1, f, 1))


def swap_lanes(value, half):
    width = value.shape[-1]
    axis = value.ndim - 1
    lane = iota(value.shape, axis)
    down = pltpu.roll(value, half, axis)
    up = pltpu.roll(value, width - half, axis)
    return jnp.where(lane // half % 2 == 0, up, down)


def stacked(refs):
    if refs[0].shape[0] % 16 == 0:
        return jnp.concatenate([ref[...] for ref in refs], 0)
    return jnp.concatenate([ref[...].astype(F32) for ref in refs], 0).astype(BF16)


def gram_kernel(share, blocks, *refs):
    pieces, out = refs[:-1], refs[-1]
    half = share * blocks
    data = stacked(pieces)
    size = data.shape[0]
    products = lax.dot_general(data, data, (((1,), (1,)), ((), ())), preferred_element_type=F32)
    if half != 8:
        row, lane = iota((size, size), 0), iota((size, size), 1)
        turned = swap_lanes(products, half)
        down, up = pltpu.roll(turned, half, 0), pltpu.roll(turned, size - half, 0)
        same = (row // half + lane // half) % 2 == 0
        out[...] = jnp.where(same, products, -products) + jnp.where(row // half % 2 == 0, up, down)
        return
    sources = size // 16
    products = products.reshape(sources, 2, 8, size)
    shape = (sources, 8, size)
    row, lane = iota(shape, 1), iota(shape, 2)
    real = products[:, 0]
    value = jnp.where(lane // half % 2 == 0, real, -real) + swap_lanes(products[:, 1], half)
    value = jnp.where(row // blocks == lane // blocks % share, value, 0.0)
    if share == 2:
        value = (value + pltpu.roll(value, 4, 1)).reshape(sources // 2, 2, 8, size)
        value = jnp.where(iota((sources // 2, 8, size), 1) < 4, value[:, 0], value[:, 1])
    out[...] = value.reshape(out.shape)


def spread_gram(value, share, blocks):
    half = share * blocks
    size = value.shape[-1]
    if half != 8:
        row, lane = iota((size, size), 0), iota((size, size), 1)
        return jnp.where(row // blocks % share == lane // blocks % share, value, 0.0)
    sources = size // 16
    shape = (sources, 8, size)
    row, lane = iota(shape, 1), iota(shape, 2)
    if share == 2:
        value = value.reshape(sources // 2, 8, size)
        other = pltpu.roll(value, 4, 1)
        low = iota(value.shape, 1) < 4
        value = jnp.stack([jnp.where(low, value, other), jnp.where(low, other, value)], 1)
    value = value.reshape(shape)
    value = jnp.where(row // blocks == lane // blocks % share, value, 0.0)
    turned = swap_lanes(value, half)
    turned = jnp.where(lane // half % 2 == 0, -turned, turned)
    return jnp.stack([value, turned], 1).reshape(size, size)


def thirds(value):
    high = value.astype(BF16)
    rest = value - high.astype(F32)
    middle = rest.astype(BF16)
    return high, middle, (rest - middle.astype(F32)).astype(BF16)


def packed_mm(left, right, full=True):
    high, middle, low = thirds(left)
    top, mid, end = right
    group = iota(left.shape, 1) // WIDTH
    terms = [top, mid, top, end]
    lanes = jnp.where(group == 2, middle, high)
    if full:
        terms += [mid, top]
        rest = jnp.where(group == 0, middle, low)[:, : 2 * WIDTH]
        lanes = jnp.concatenate([lanes, rest], 1)
    return jnp.dot(lanes, jnp.concatenate(terms, 0), preferred_element_type=F32)


def inverse_roots(inners, lefts, rights):
    shape = inners[0].shape
    identity = jnp.where(iota(shape, 0) == iota(shape, 1) % WIDTH, 1.0, 0.0)
    squares = [packed_mm(inner, thirds(inner)) for inner in inners]
    norms = [
        jnp.sqrt(jnp.sum(inner * inner, keepdims=True) * (1.0 / COPIES)) for inner in inners
    ]
    scales = [1.0 / norm for norm in norms]
    rests = [identity - inner * scale for inner, scale in zip(inners, scales)]
    squares = [
        2.0 * rest - identity + square * scale * scale
        for rest, square, scale in zip(rests, squares, scales)
    ]
    roots = None
    for step in range(NS_STEPS - 1):
        full = step < FULL_STEPS
        terms = [thirds(rest) for rest in rests]
        if step > 0:
            squares = [packed_mm(e, r, full) for e, r in zip(rests, terms)]
            roots = [z + 0.5 * packed_mm(z, r, full) for z, r in zip(roots, terms)]
        else:
            roots = [identity + 0.5 * e for e in rests]
        cubes = [packed_mm(s, r, full) for s, r in zip(squares, terms)]
        rests = [0.75 * s + 0.25 * c for s, c in zip(squares, cubes)]
    scales = [1.0 / jnp.sqrt(norm) for norm in norms]
    lefts = [packed_mm(z, thirds(left)) for z, left in zip(roots, lefts)]
    rights = [packed_mm(right, thirds(z)) for z, right in zip(roots, rights)]
    lefts = [
        (left + 0.5 * packed_mm(e, thirds(left), False)) * scale
        for e, left, scale in zip(rests, lefts, scales)
    ]
    rights = [
        (right + 0.5 * packed_mm(right, thirds(e), False)) * scale
        for e, right, scale in zip(rests, rights, scales)
    ]
    return lefts, rights


def subspace_kernel(share, blocks, dofs, grams, *refs):
    parts, (wide, tall, coef_out, energy_out) = refs[:grams], refs[grams:]
    value = parts[0][...]
    for part in parts[1:]:
        value = value + part[...]
    gram = spread_gram(value * (1.0 / dofs), share, blocks)
    freqs = range(share)
    tall_next = mm(tall[...], gram)
    images = [mm(gram, mm(gram, wide[f])) for f in freqs]
    rows = [tall_next[f * WIDTH : (f + 1) * WIDTH] for f in freqs]
    for _ in range(ITERS - 1):
        inners = [mm(rows[f], images[f]) for f in freqs]
        tall_image = mm(jnp.concatenate(rows, 0), gram)
        ahead = [mm(gram, image) for image in images]
        rows = [tall_image[f * WIDTH : (f + 1) * WIDTH] for f in freqs]
        rows, images = inverse_roots(inners, rows, ahead)
    inners = [mm(rows[f], images[f]) for f in freqs]
    coefs, finals = inverse_roots(inners, rows, images)
    half = share * blocks
    me = lax.axis_index("blk")
    energy_out[...] = jnp.zeros_like(energy_out)
    for f, (coef, final) in enumerate(zip(coefs, finals)):
        energy = jnp.sum(final * final, axis=0, keepdims=True)
        energy_out[pl.ds(me * share + f, 1), :] = energy[:, :RANK]
        same = (iota(coef.shape, 0) // RANK + iota(coef.shape, 1) // half) % 2 == 0
        coef_out[f * WIDTH : (f + 1) * WIDTH] = jnp.where(same, coef, -coef).astype(BF16)


def modes_kernel(share, quad, coef, *refs):
    pieces, out = refs[:-1], refs[-1]
    data = stacked(pieces)
    points = quad.shape[-1]
    inverse = 1.0 / jnp.sqrt(quad[...])
    for c in range(data.shape[-1] // points):
        modes = inverse * jnp.dot(
            coef[...], data[:, c * points : (c + 1) * points], preferred_element_type=F32
        )
        for f in range(share):
            for part in range(2):
                at = (2 * f + part) * RANK
                out[f, part, c] = modes[at : at + RANK]


def call(kernel, outs, specs, name, scratch=()):
    return pl.pallas_call(
        kernel,
        out_shape=outs,
        in_specs=specs,
        out_specs=jax.tree.map(lambda _: VMEM, outs),
        scratch_shapes=list(scratch),
        compiler_params=pltpu.CompilerParams(vmem_limit_bytes=LIMIT),
        name=name,
    )


def exchange(array, axis, distance):
    size = lax.axis_size(axis)
    return lax.ppermute(array, axis, [(i, i ^ distance) for i in range(size)])


def per_device(snapshots, quadrature, omega):
    blocks, samples, comps, points = snapshots.shape
    groups, spaces = lax.axis_size("blk"), lax.axis_size("space")
    share = NF // groups
    reach = groups // 2
    height = 2 * share * blocks
    width = comps * points
    size = groups * height
    piece = (height, width)

    table = in_hbm(jnp.asarray(table_rows(samples, groups)))
    quad = quadrature.reshape(1, points)
    steps = blocks * comps
    spectra = call(
        functools.partial(spectra_kernel, groups),
        [jax.ShapeDtypeStruct((2, *piece), BF16)] * reach,
        [HBM] * 3,
        "spectra",
        [
            pltpu.VMEM((blocks, comps, samples, points), BF16),
            pltpu.VMEM(table.shape, BF16),
            pltpu.VMEM((1, points), F32),
            pltpu.VMEM((size, blocks * samples), BF16),
            pltpu.VMEM((groups, *piece), BF16),
            pltpu.SemaphoreType.DMA((steps,)),
            pltpu.SemaphoreType.DMA((2,)),
        ],
    )(in_hbm(snapshots.transpose(0, 2, 1, 3)), table, in_hbm(quad))

    wide, tall = call(
        functools.partial(start_kernel, share, blocks),
        [
            jax.ShapeDtypeStruct((share, size, COPIES * WIDTH), F32),
            jax.ShapeDtypeStruct((share * WIDTH, size), F32),
        ],
        [HBM, pl.BlockSpec(memory_space=pl.ANY)],
        "start",
        [pltpu.VMEM((share, 2, RANK, groups * blocks), F32), pltpu.SemaphoreType.DMA],
    )(in_hbm(omega.transpose(0, 1, 3, 2)), spectra[0])

    arrived = {far: exchange(spectra[far], "blk", 2 * far) for far in range(1, reach)}
    wide, tall, arrived[1] = lax.optimization_barrier((wide, tall, arrived[1]))
    arrived[0] = spectra[0]
    others = {}
    for part in (range(1, reach, 2), range(0, reach, 2)):
        sent = exchange(jnp.stack([arrived[far][1] for far in part]), "blk", 1)
        others |= {far: sent[i] for i, far in enumerate(part)}
    pieces = [piece for far in range(reach) for piece in (arrived[far][0], others[far])]

    packed = (size * (blocks if share * blocks == 8 else height) // height, size)
    gram = call(
        functools.partial(gram_kernel, share, blocks),
        jax.ShapeDtypeStruct(packed, F32),
        [VMEM] * groups,
        "gram",
    )(*pieces)
    if spaces <= 4:
        grams = [gram] + [exchange(gram, "space", d) for d in range(1, spaces)]
    else:
        grams = [lax.psum(gram, "space")]

    coef, energies = call(
        functools.partial(subspace_kernel, share, blocks, width * spaces, len(grams)),
        [
            jax.ShapeDtypeStruct((share * WIDTH, size), BF16),
            jax.ShapeDtypeStruct((NF, RANK), F32),
        ],
        [VMEM] * (len(grams) + 2),
        "subspace",
    )(*grams, wide, tall)

    modes = call(
        functools.partial(modes_kernel, share),
        jax.ShapeDtypeStruct((share, 2, comps, RANK, points), F32),
        [VMEM] * (groups + 2),
        "modes",
    )(quad, coef, *pieces)

    energies = energies + exchange(energies, "blk", 1)
    shares = [exchange(energies, "blk", 2 * far) for far in range(1, reach)]
    for other in shares:
        energies = energies + other
    return modes.transpose(0, 1, 3, 2, 4), energies


def solution(mesh):
    in_specs = (P("blk", None, None, "space"), P("space"), P())
    out_specs = (P("blk", None, None, None, "space"), P())
    return jax.shard_map(
        per_device, mesh=mesh, in_specs=in_specs, out_specs=out_specs, check_vma=False
    )
```

```python
import functools
import math

import jax
import jax.numpy as jnp
import ml_dtypes
import numpy as np
from jax import lax
from jax.experimental import pallas as pl
from jax.experimental.pallas import tpu as pltpu
from jax.sharding import PartitionSpec as P

NF = 16
RANK = 16
ITERS = 2
NS_STEPS = 14
FULL_STEPS = 6
WIDTH = 2 * RANK
COPIES = 4
IN_FLIGHT = 8
LIMIT = 40 * 2**20
F32, BF16 = jnp.float32, jnp.bfloat16
HBM = pl.BlockSpec(memory_space=pltpu.HBM)
VMEM = pl.BlockSpec(memory_space=pltpu.VMEM)


def in_hbm(array):
    return pltpu.with_memory_space_constraint(array, pltpu.HBM)


def dft_table(sample_count, harmonic_count):
    sample = np.arange(sample_count, dtype=np.int32)
    harmonic = np.arange(1, harmonic_count + 1, dtype=np.int32)
    turns = harmonic[:, None] * sample[None, :] % sample_count
    phases = np.float32(2.0 * math.pi / sample_count) * turns.astype(np.float32)
    window = np.float32(0.5) - np.float32(0.5) * np.cos(
        np.float32(2.0 * math.pi / sample_count) * sample.astype(np.float32)
    )
    factor = np.float32(1.0) / np.sqrt(np.sum(window * window, dtype=np.float32))
    return np.stack([window * np.cos(phases) * factor, -window * np.sin(phases) * factor])


def table_rows(sample_count, groups):
    rows = dft_table(sample_count, NF).reshape(2, groups, NF // groups, sample_count)
    rows = rows.transpose(1, 0, 2, 3).reshape(2 * NF, sample_count)
    return rows.astype(ml_dtypes.bfloat16)


def iota(shape, axis):
    return lax.broadcasted_iota(jnp.int32, shape, axis)


def mm(left, right, contract=(1, 0)):
    dims = (((contract[0],), (contract[1],)), ((), ()))
    return lax.dot_general(
        left, right, dims, precision=lax.Precision.HIGHEST, preferred_element_type=F32
    )


def spectra_kernel(groups, snap, table_hbm, quad_hbm, *refs):
    outs, (buf, thin, quad, table, piles, sems, small) = refs[:-7], refs[-7:]
    blocks, comps, samples, points = snap.shape
    steps = [(c, b) for c in range(comps) for b in range(blocks)]
    copies = [
        pltpu.make_async_copy(snap.at[b, c], buf.at[b, c], sems.at[i])
        for i, (c, b) in enumerate(steps)
    ]
    table_copy = pltpu.make_async_copy(table_hbm, thin, small.at[0])
    quad_copy = pltpu.make_async_copy(quad_hbm, quad, small.at[1])
    table_copy.start()
    quad_copy.start()
    for i, copy in enumerate(copies[:IN_FLIGHT]):
        copy.start(priority=int(i < blocks))
    me = lax.axis_index("blk")
    height = piles.shape[1]
    table_copy.wait()
    shape = (table.shape[0], thin.shape[0])
    spread = jnp.where(iota(shape, 0) // blocks == iota(shape, 1), 1.0, 0.0).astype(BF16)
    spread = jnp.dot(spread, thin[...], preferred_element_type=F32)
    for b in range(blocks):
        table[:, b * samples : (b + 1) * samples] = jnp.where(
            iota(spread.shape, 0) % blocks == b, spread, 0.0
        ).astype(BF16)
    quad_copy.wait()
    root = jnp.sqrt(quad[...])
    for i, (c, b) in enumerate(steps):
        copies[i].wait()
        if i + IN_FLIGHT < len(copies):
            copies[i + IN_FLIGHT].start()
        part = jnp.dot(
            table[:, b * samples : (b + 1) * samples], buf[b, c], preferred_element_type=F32
        )
        total = part if b == 0 else total + part
        if b == blocks - 1:
            low = (total * root).astype(BF16)
            for owner in range(groups):
                piles[owner, :, c * points : (c + 1) * points] = low[
                    owner * height : (owner + 1) * height
                ]
    for far, out in enumerate(outs):
        for core in range(2):
            out[core] = piles[me ^ (2 * far + core)]


def start_kernel(share, blocks, omega, _, wide_out, tall_out, own, sem):
    me = lax.axis_index("blk")
    copy = pltpu.make_async_copy(omega.at[pl.ds(me * share, share)], own, sem)
    copy.start()
    copy.wait()
    total = own.shape[-1]
    half = share * blocks
    size = 2 * share * total

    def placed(shape, axis, f, part):
        index, block = iota(shape, axis), iota(shape, 1 - axis)
        same = ((index // (2 * half)) ^ me) * blocks + index % blocks == block
        return jnp.where(same & (index // blocks % share == f) & (index // half % 2 == part), 1.0, 0.0)

    for f in range(share):
        real, imag = own[f, 0], own[f, 1]
        first = jnp.concatenate([real, -imag], 0)
        second = jnp.concatenate([imag, real], 0)
        wide_out[f] = mm(
            placed((size, total), 0, f, 0), jnp.concatenate([first] * COPIES, 0), (1, 1)
        ) + mm(placed((size, total), 0, f, 1), jnp.concatenate([second] * COPIES, 0), (1, 1))
        tall_out[f * WIDTH : (f + 1) * WIDTH] = mm(
            first, placed((total, size), 1, f, 0)
        ) + mm(second, placed((total, size), 1, f, 1))


def swap_lanes(value, half):
    width = value.shape[-1]
    axis = value.ndim - 1
    lane = iota(value.shape, axis)
    down = pltpu.roll(value, half, axis)
    up = pltpu.roll(value, width - half, axis)
    return jnp.where(lane // half % 2 == 0, up, down)


def stacked(refs):
    if refs[0].shape[0] % 16 == 0:
        return jnp.concatenate([ref[...] for ref in refs], 0)
    return jnp.concatenate([ref[...].astype(F32) for ref in refs], 0).astype(BF16)


def gram_kernel(share, blocks, *refs):
    pieces, out = refs[:-1], refs[-1]
    half = share * blocks
    data = stacked(pieces)
    size = data.shape[0]
    products = lax.dot_general(data, data, (((1,), (1,)), ((), ())), preferred_element_type=F32)
    if half != 8:
        row, lane = iota((size, size), 0), iota((size, size), 1)
        turned = swap_lanes(products, half)
        down, up = pltpu.roll(turned, half, 0), pltpu.roll(turned, size - half, 0)
        same = (row // half + lane // half) % 2 == 0
        out[...] = jnp.where(same, products, -products) + jnp.where(row // half % 2 == 0, up, down)
        return
    sources = size // 16
    products = products.reshape(sources, 2, 8, size)
    shape = (sources, 8, size)
    row, lane = iota(shape, 1), iota(shape, 2)
    real = products[:, 0]
    value = jnp.where(lane // half % 2 == 0, real, -real) + swap_lanes(products[:, 1], half)
    value = jnp.where(row // blocks == lane // blocks % share, value, 0.0)
    if share == 2:
        value = (value + pltpu.roll(value, 4, 1)).reshape(sources // 2, 2, 8, size)
        value = jnp.where(iota((sources // 2, 8, size), 1) < 4, value[:, 0], value[:, 1])
    out[...] = value.reshape(out.shape)


def spread_gram(value, share, blocks):
    half = share * blocks
    size = value.shape[-1]
    if half != 8:
        row, lane = iota((size, size), 0), iota((size, size), 1)
        return jnp.where(row // blocks % share == lane // blocks % share, value, 0.0)
    sources = size // 16
    shape = (sources, 8, size)
    row, lane = iota(shape, 1), iota(shape, 2)
    if share == 2:
        value = value.reshape(sources // 2, 8, size)
        other = pltpu.roll(value, 4, 1)
        low = iota(value.shape, 1) < 4
        value = jnp.stack([jnp.where(low, value, other), jnp.where(low, other, value)], 1)
    value = value.reshape(shape)
    value = jnp.where(row // blocks == lane // blocks % share, value, 0.0)
    turned = swap_lanes(value, half)
    turned = jnp.where(lane // half % 2 == 0, -turned, turned)
    return jnp.stack([value, turned], 1).reshape(size, size)


def thirds(value):
    high = value.astype(BF16)
    rest = value - high.astype(F32)
    middle = rest.astype(BF16)
    return high, middle, (rest - middle.astype(F32)).astype(BF16)


def packed_mm(left, right, full=True):
    high, middle, low = thirds(left)
    top, mid, end = right
    group = iota(left.shape, 1) // WIDTH
    terms = [top, mid, top, end]
    lanes = jnp.where(group == 2, middle, high)
    if full:
        terms += [mid, top]
        rest = jnp.where(group == 0, middle, low)[:, : 2 * WIDTH]
        lanes = jnp.concatenate([lanes, rest], 1)
    return jnp.dot(lanes, jnp.concatenate(terms, 0), preferred_element_type=F32)


def inverse_roots(inners, lefts, rights):
    shape = inners[0].shape
    identity = jnp.where(iota(shape, 0) == iota(shape, 1) % WIDTH, 1.0, 0.0)
    squares = [packed_mm(inner, thirds(inner)) for inner in inners]
    norms = [
        jnp.sqrt(jnp.sum(inner * inner, keepdims=True) * (1.0 / COPIES)) for inner in inners
    ]
    scales = [1.0 / norm for norm in norms]
    rests = [identity - inner * scale for inner, scale in zip(inners, scales)]
    squares = [
        2.0 * rest - identity + square * scale * scale
        for rest, square, scale in zip(rests, squares, scales)
    ]
    roots = None
    for step in range(NS_STEPS - 1):
        full = step < FULL_STEPS
        terms = [thirds(rest) for rest in rests]
        if step > 0:
            squares = [packed_mm(e, r, full) for e, r in zip(rests, terms)]
            roots = [z + 0.5 * packed_mm(z, r, full) for z, r in zip(roots, terms)]
        else:
            roots = [identity + 0.5 * e for e in rests]
        cubes = [packed_mm(s, r, full) for s, r in zip(squares, terms)]
        rests = [0.75 * s + 0.25 * c for s, c in zip(squares, cubes)]
    scales = [1.0 / jnp.sqrt(norm) for norm in norms]
    lefts = [packed_mm(z, thirds(left)) for z, left in zip(roots, lefts)]
    rights = [packed_mm(right, thirds(z)) for z, right in zip(roots, rights)]
    lefts = [
        (left + 0.5 * packed_mm(e, thirds(left), False)) * scale
        for e, left, scale in zip(rests, lefts, scales)
    ]
    rights = [
        (right + 0.5 * packed_mm(right, thirds(e), False)) * scale
        for e, right, scale in zip(rests, rights, scales)
    ]
    return lefts, rights


def subspace_kernel(share, blocks, dofs, grams, *refs):
    parts, (wide, tall, coef_out, energy_out) = refs[:grams], refs[grams:]
    value = parts[0][...]
    for part in parts[1:]:
        value = value + part[...]
    gram = spread_gram(value * (1.0 / dofs), share, blocks)
    freqs = range(share)
    tall_next = mm(tall[...], gram)
    images = [mm(gram, mm(gram, wide[f])) for f in freqs]
    rows = [tall_next[f * WIDTH : (f + 1) * WIDTH] for f in freqs]
    for _ in range(ITERS - 1):
        inners = [mm(rows[f], images[f]) for f in freqs]
        tall_image = mm(jnp.concatenate(rows, 0), gram)
        ahead = [mm(gram, image) for image in images]
        rows = [tall_image[f * WIDTH : (f + 1) * WIDTH] for f in freqs]
        rows, images = inverse_roots(inners, rows, ahead)
    inners = [mm(rows[f], images[f]) for f in freqs]
    coefs, finals = inverse_roots(inners, rows, images)
    half = share * blocks
    me = lax.axis_index("blk")
    energy_out[...] = jnp.zeros_like(energy_out)
    for f, (coef, final) in enumerate(zip(coefs, finals)):
        energy = jnp.sum(final * final, axis=0, keepdims=True)
        energy_out[pl.ds(me * share + f, 1), :] = energy[:, :RANK]
        same = (iota(coef.shape, 0) // RANK + iota(coef.shape, 1) // half) % 2 == 0
        coef_out[f * WIDTH : (f + 1) * WIDTH] = jnp.where(same, coef, -coef).astype(BF16)


def modes_kernel(share, quad, coef, *refs):
    pieces, out = refs[:-1], refs[-1]
    data = stacked(pieces)
    points = quad.shape[-1]
    inverse = 1.0 / jnp.sqrt(quad[...])
    for c in range(data.shape[-1] // points):
        modes = inverse * jnp.dot(
            coef[...], data[:, c * points : (c + 1) * points], preferred_element_type=F32
        )
        for f in range(share):
            for part in range(2):
                at = (2 * f + part) * RANK
                out[f, part, c] = modes[at : at + RANK]


def call(kernel, outs, specs, name, scratch=()):
    return pl.pallas_call(
        kernel,
        out_shape=outs,
        in_specs=specs,
        out_specs=jax.tree.map(lambda _: VMEM, outs),
        scratch_shapes=list(scratch),
        compiler_params=pltpu.CompilerParams(vmem_limit_bytes=LIMIT),
        name=name,
    )


def exchange(array, axis, distance):
    size = lax.axis_size(axis)
    return lax.ppermute(array, axis, [(i, i ^ distance) for i in range(size)])


def per_device(snapshots, quadrature, omega):
    blocks, samples, comps, points = snapshots.shape
    groups, spaces = lax.axis_size("blk"), lax.axis_size("space")
    share = NF // groups
    reach = groups // 2
    height = 2 * share * blocks
    width = comps * points
    size = groups * height
    piece = (height, width)

    table = in_hbm(jnp.asarray(table_rows(samples, groups)))
    quad = quadrature.reshape(1, points)
    steps = blocks * comps
    spectra = call(
        functools.partial(spectra_kernel, groups),
        [jax.ShapeDtypeStruct((2, *piece), BF16)] * reach,
        [HBM] * 3,
        "spectra",
        [
            pltpu.VMEM((blocks, comps, samples, points), BF16),
            pltpu.VMEM(table.shape, BF16),
            pltpu.VMEM((1, points), F32),
            pltpu.VMEM((size, blocks * samples), BF16),
            pltpu.VMEM((groups, *piece), BF16),
            pltpu.SemaphoreType.DMA((steps,)),
            pltpu.SemaphoreType.DMA((2,)),
        ],
    )(in_hbm(snapshots.transpose(0, 2, 1, 3)), table, in_hbm(quad))

    wide, tall = call(
        functools.partial(start_kernel, share, blocks),
        [
            jax.ShapeDtypeStruct((share, size, COPIES * WIDTH), F32),
            jax.ShapeDtypeStruct((share * WIDTH, size), F32),
        ],
        [HBM, pl.BlockSpec(memory_space=pl.ANY)],
        "start",
        [pltpu.VMEM((share, 2, RANK, groups * blocks), F32), pltpu.SemaphoreType.DMA],
    )(in_hbm(omega.transpose(0, 1, 3, 2)), spectra[0])

    arrived = {far: exchange(spectra[far], "blk", 2 * far) for far in range(1, reach)}
    wide, tall, arrived[1] = lax.optimization_barrier((wide, tall, arrived[1]))
    arrived[0] = spectra[0]
    others = {}
    for part in (range(1, reach, 2), range(0, reach, 2)):
        sent = exchange(jnp.stack([arrived[far][1] for far in part]), "blk", 1)
        others |= {far: sent[i] for i, far in enumerate(part)}
    pieces = [piece for far in range(reach) for piece in (arrived[far][0], others[far])]

    packed = (size * (blocks if share * blocks == 8 else height) // height, size)
    gram = call(
        functools.partial(gram_kernel, share, blocks),
        jax.ShapeDtypeStruct(packed, F32),
        [VMEM] * groups,
        "gram",
    )(*pieces)
    if spaces <= 4:
        grams = [gram] + [exchange(gram, "space", d) for d in range(1, spaces)]
    else:
        grams = [lax.psum(gram, "space")]

    coef, energies = call(
        functools.partial(subspace_kernel, share, blocks, width * spaces, len(grams)),
        [
            jax.ShapeDtypeStruct((share * WIDTH, size), BF16),
            jax.ShapeDtypeStruct((NF, RANK), F32),
        ],
        [VMEM] * (len(grams) + 2),
        "subspace",
    )(*grams, wide, tall)

    modes = call(
        functools.partial(modes_kernel, share),
        jax.ShapeDtypeStruct((share, 2, comps, RANK, points), F32),
        [VMEM] * (groups + 2),
        "modes",
    )(quad, coef, *pieces)

    energies = energies + exchange(energies, "blk", 1)
    shares = [exchange(energies, "blk", 2 * far) for far in range(1, reach)]
    for other in shares:
        energies = energies + other
    return modes.transpose(0, 1, 3, 2, 4), energies


def solution(mesh):
    in_specs = (P("blk", None, None, "space"), P("space"), P())
    out_specs = (P("blk", None, None, None, "space"), P())
    return jax.shard_map(
        per_device, mesh=mesh, in_specs=in_specs, out_specs=out_specs, check_vma=False
    )
```

```python
import functools
import math

import jax
import jax.numpy as jnp
import ml_dtypes
import numpy as np
from jax import lax
from jax.experimental import pallas as pl
from jax.experimental.pallas import tpu as pltpu
from jax.sharding import PartitionSpec as P

NF = 16
RANK = 16
ITERS = 2
NS_STEPS = 14
FULL_STEPS = 6
WIDTH = 2 * RANK
COPIES = 4
IN_FLIGHT = 8
LIMIT = 40 * 2**20
F32, BF16 = jnp.float32, jnp.bfloat16
HBM = pl.BlockSpec(memory_space=pltpu.HBM)
VMEM = pl.BlockSpec(memory_space=pltpu.VMEM)


def in_hbm(array):
    return pltpu.with_memory_space_constraint(array, pltpu.HBM)


def dft_table(sample_count, harmonic_count):
    sample = np.arange(sample_count, dtype=np.int32)
    harmonic = np.arange(1, harmonic_count + 1, dtype=np.int32)
    turns = harmonic[:, None] * sample[None, :] % sample_count
    phases = np.float32(2.0 * math.pi / sample_count) * turns.astype(np.float32)
    window = np.float32(0.5) - np.float32(0.5) * np.cos(
        np.float32(2.0 * math.pi / sample_count) * sample.astype(np.float32)
    )
    factor = np.float32(1.0) / np.sqrt(np.sum(window * window, dtype=np.float32))
    return np.stack([window * np.cos(phases) * factor, -window * np.sin(phases) * factor])


def table_rows(sample_count, groups):
    rows = dft_table(sample_count, NF).reshape(2, groups, NF // groups, sample_count)
    rows = rows.transpose(1, 0, 2, 3).reshape(2 * NF, sample_count)
    return rows.astype(ml_dtypes.bfloat16)


def iota(shape, axis):
    return lax.broadcasted_iota(jnp.int32, shape, axis)


def mm(left, right, contract=(1, 0)):
    dims = (((contract[0],), (contract[1],)), ((), ()))
    return lax.dot_general(
        left, right, dims, precision=lax.Precision.HIGHEST, preferred_element_type=F32
    )


def spectra_kernel(groups, snap, table_hbm, quad_hbm, *refs):
    outs, (buf, thin, quad, table, piles, sems, small) = refs[:-7], refs[-7:]
    blocks, comps, samples, points = snap.shape
    steps = [(c, b) for c in range(comps) for b in range(blocks)]
    copies = [
        pltpu.make_async_copy(snap.at[b, c], buf.at[b, c], sems.at[i])
        for i, (c, b) in enumerate(steps)
    ]
    table_copy = pltpu.make_async_copy(table_hbm, thin, small.at[0])
    quad_copy = pltpu.make_async_copy(quad_hbm, quad, small.at[1])
    table_copy.start()
    quad_copy.start()
    for i, copy in enumerate(copies[:IN_FLIGHT]):
        copy.start(priority=int(i < 6))
    me = lax.axis_index("blk")
    height = piles.shape[1]
    table_copy.wait()
    shape = (table.shape[0], thin.shape[0])
    spread = jnp.where(iota(shape, 0) // blocks == iota(shape, 1), 1.0, 0.0).astype(BF16)
    spread = jnp.dot(spread, thin[...], preferred_element_type=F32)
    for b in range(blocks):
        table[:, b * samples : (b + 1) * samples] = jnp.where(
            iota(spread.shape, 0) % blocks == b, spread, 0.0
        ).astype(BF16)
    quad_copy.wait()
    root = jnp.sqrt(quad[...])
    for i, (c, b) in enumerate(steps):
        copies[i].wait()
        if i + IN_FLIGHT < len(copies):
            copies[i + IN_FLIGHT].start()
        part = jnp.dot(
            table[:, b * samples : (b + 1) * samples], buf[b, c], preferred_element_type=F32
        )
        total = part if b == 0 else total + part
        if b == blocks - 1:
            low = (total * root).astype(BF16)
            for owner in range(groups):
                piles[owner, :, c * points : (c + 1) * points] = low[
                    owner * height : (owner + 1) * height
                ]
    for far, out in enumerate(outs):
        for core in range(2):
            out[core] = piles[me ^ (2 * far + core)]


def start_kernel(share, blocks, omega, _, wide_out, tall_out, own, sem):
    me = lax.axis_index("blk")
    copy = pltpu.make_async_copy(omega.at[pl.ds(me * share, share)], own, sem)
    copy.start()
    copy.wait()
    total = own.shape[-1]
    half = share * blocks
    size = 2 * share * total

    def placed(shape, axis, f, part):
        index, block = iota(shape, axis), iota(shape, 1 - axis)
        same = ((index // (2 * half)) ^ me) * blocks + index % blocks == block
        return jnp.where(same & (index // blocks % share == f) & (index // half % 2 == part), 1.0, 0.0)

    for f in range(share):
        real, imag = own[f, 0], own[f, 1]
        first = jnp.concatenate([real, -imag], 0)
        second = jnp.concatenate([imag, real], 0)
        wide_out[f] = mm(
            placed((size, total), 0, f, 0), jnp.concatenate([first] * COPIES, 0), (1, 1)
        ) + mm(placed((size, total), 0, f, 1), jnp.concatenate([second] * COPIES, 0), (1, 1))
        tall_out[f * WIDTH : (f + 1) * WIDTH] = mm(
            first, placed((total, size), 1, f, 0)
        ) + mm(second, placed((total, size), 1, f, 1))


def swap_lanes(value, half):
    width = value.shape[-1]
    axis = value.ndim - 1
    lane = iota(value.shape, axis)
    down = pltpu.roll(value, half, axis)
    up = pltpu.roll(value, width - half, axis)
    return jnp.where(lane // half % 2 == 0, up, down)


def stacked(refs):
    if refs[0].shape[0] % 16 == 0:
        return jnp.concatenate([ref[...] for ref in refs], 0)
    return jnp.concatenate([ref[...].astype(F32) for ref in refs], 0).astype(BF16)


def gram_kernel(share, blocks, *refs):
    pieces, out = refs[:-1], refs[-1]
    half = share * blocks
    data = stacked(pieces)
    size = data.shape[0]
    products = lax.dot_general(data, data, (((1,), (1,)), ((), ())), preferred_element_type=F32)
    if half != 8:
        row, lane = iota((size, size), 0), iota((size, size), 1)
        turned = swap_lanes(products, half)
        down, up = pltpu.roll(turned, half, 0), pltpu.roll(turned, size - half, 0)
        same = (row // half + lane // half) % 2 == 0
        out[...] = jnp.where(same, products, -products) + jnp.where(row // half % 2 == 0, up, down)
        return
    sources = size // 16
    products = products.reshape(sources, 2, 8, size)
    shape = (sources, 8, size)
    row, lane = iota(shape, 1), iota(shape, 2)
    real = products[:, 0]
    value = jnp.where(lane // half % 2 == 0, real, -real) + swap_lanes(products[:, 1], half)
    value = jnp.where(row // blocks == lane // blocks % share, value, 0.0)
    if share == 2:
        value = (value + pltpu.roll(value, 4, 1)).reshape(sources // 2, 2, 8, size)
        value = jnp.where(iota((sources // 2, 8, size), 1) < 4, value[:, 0], value[:, 1])
    out[...] = value.reshape(out.shape)


def spread_gram(value, share, blocks):
    half = share * blocks
    size = value.shape[-1]
    if half != 8:
        row, lane = iota((size, size), 0), iota((size, size), 1)
        return jnp.where(row // blocks % share == lane // blocks % share, value, 0.0)
    sources = size // 16
    shape = (sources, 8, size)
    row, lane = iota(shape, 1), iota(shape, 2)
    if share == 2:
        value = value.reshape(sources // 2, 8, size)
        other = pltpu.roll(value, 4, 1)
        low = iota(value.shape, 1) < 4
        value = jnp.stack([jnp.where(low, value, other), jnp.where(low, other, value)], 1)
    value = value.reshape(shape)
    value = jnp.where(row // blocks == lane // blocks % share, value, 0.0)
    turned = swap_lanes(value, half)
    turned = jnp.where(lane // half % 2 == 0, -turned, turned)
    return jnp.stack([value, turned], 1).reshape(size, size)


def thirds(value):
    high = value.astype(BF16)
    rest = value - high.astype(F32)
    middle = rest.astype(BF16)
    return high, middle, (rest - middle.astype(F32)).astype(BF16)


def packed_mm(left, right, full=True):
    high, middle, low = thirds(left)
    top, mid, end = right
    group = iota(left.shape, 1) // WIDTH
    terms = [top, mid, top, end]
    lanes = jnp.where(group == 2, middle, high)
    if full:
        terms += [mid, top]
        rest = jnp.where(group == 0, middle, low)[:, : 2 * WIDTH]
        lanes = jnp.concatenate([lanes, rest], 1)
    return jnp.dot(lanes, jnp.concatenate(terms, 0), preferred_element_type=F32)


def inverse_roots(inners, lefts, rights):
    shape = inners[0].shape
    identity = jnp.where(iota(shape, 0) == iota(shape, 1) % WIDTH, 1.0, 0.0)
    squares = [packed_mm(inner, thirds(inner)) for inner in inners]
    norms = [
        jnp.sqrt(jnp.sum(inner * inner, keepdims=True) * (1.0 / COPIES)) for inner in inners
    ]
    scales = [1.0 / norm for norm in norms]
    rests = [identity - inner * scale for inner, scale in zip(inners, scales)]
    squares = [
        2.0 * rest - identity + square * scale * scale
        for rest, square, scale in zip(rests, squares, scales)
    ]
    roots = None
    for step in range(NS_STEPS - 1):
        full = step < FULL_STEPS
        terms = [thirds(rest) for rest in rests]
        if step > 0:
            squares = [packed_mm(e, r, full) for e, r in zip(rests, terms)]
            roots = [z + 0.5 * packed_mm(z, r, full) for z, r in zip(roots, terms)]
        else:
            roots = [identity + 0.5 * e for e in rests]
        cubes = [packed_mm(s, r, full) for s, r in zip(squares, terms)]
        rests = [0.75 * s + 0.25 * c for s, c in zip(squares, cubes)]
    scales = [1.0 / jnp.sqrt(norm) for norm in norms]
    lefts = [packed_mm(z, thirds(left)) for z, left in zip(roots, lefts)]
    rights = [packed_mm(right, thirds(z)) for z, right in zip(roots, rights)]
    lefts = [
        (left + 0.5 * packed_mm(e, thirds(left), False)) * scale
        for e, left, scale in zip(rests, lefts, scales)
    ]
    rights = [
        (right + 0.5 * packed_mm(right, thirds(e), False)) * scale
        for e, right, scale in zip(rests, rights, scales)
    ]
    return lefts, rights


def subspace_kernel(share, blocks, dofs, grams, *refs):
    parts, (wide, tall, coef_out, energy_out) = refs[:grams], refs[grams:]
    value = parts[0][...]
    for part in parts[1:]:
        value = value + part[...]
    gram = spread_gram(value * (1.0 / dofs), share, blocks)
    freqs = range(share)
    tall_next = mm(tall[...], gram)
    images = [mm(gram, mm(gram, wide[f])) for f in freqs]
    rows = [tall_next[f * WIDTH : (f + 1) * WIDTH] for f in freqs]
    for _ in range(ITERS - 1):
        inners = [mm(rows[f], images[f]) for f in freqs]
        tall_image = mm(jnp.concatenate(rows, 0), gram)
        ahead = [mm(gram, image) for image in images]
        rows = [tall_image[f * WIDTH : (f + 1) * WIDTH] for f in freqs]
        rows, images = inverse_roots(inners, rows, ahead)
    inners = [mm(rows[f], images[f]) for f in freqs]
    coefs, finals = inverse_roots(inners, rows, images)
    half = share * blocks
    me = lax.axis_index("blk")
    energy_out[...] = jnp.zeros_like(energy_out)
    for f, (coef, final) in enumerate(zip(coefs, finals)):
        energy = jnp.sum(final * final, axis=0, keepdims=True)
        energy_out[pl.ds(me * share + f, 1), :] = energy[:, :RANK]
        same = (iota(coef.shape, 0) // RANK + iota(coef.shape, 1) // half) % 2 == 0
        coef_out[f * WIDTH : (f + 1) * WIDTH] = jnp.where(same, coef, -coef).astype(BF16)


def modes_kernel(share, quad, coef, *refs):
    pieces, out = refs[:-1], refs[-1]
    data = stacked(pieces)
    points = quad.shape[-1]
    inverse = 1.0 / jnp.sqrt(quad[...])
    for c in range(data.shape[-1] // points):
        modes = inverse * jnp.dot(
            coef[...], data[:, c * points : (c + 1) * points], preferred_element_type=F32
        )
        for f in range(share):
            for part in range(2):
                at = (2 * f + part) * RANK
                out[f, part, c] = modes[at : at + RANK]


def call(kernel, outs, specs, name, scratch=()):
    return pl.pallas_call(
        kernel,
        out_shape=outs,
        in_specs=specs,
        out_specs=jax.tree.map(lambda _: VMEM, outs),
        scratch_shapes=list(scratch),
        compiler_params=pltpu.CompilerParams(vmem_limit_bytes=LIMIT),
        name=name,
    )


def exchange(array, axis, distance):
    size = lax.axis_size(axis)
    return lax.ppermute(array, axis, [(i, i ^ distance) for i in range(size)])


def per_device(snapshots, quadrature, omega):
    blocks, samples, comps, points = snapshots.shape
    groups, spaces = lax.axis_size("blk"), lax.axis_size("space")
    share = NF // groups
    reach = groups // 2
    height = 2 * share * blocks
    width = comps * points
    size = groups * height
    piece = (height, width)

    table = in_hbm(jnp.asarray(table_rows(samples, groups)))
    quad = quadrature.reshape(1, points)
    steps = blocks * comps
    spectra = call(
        functools.partial(spectra_kernel, groups),
        [jax.ShapeDtypeStruct((2, *piece), BF16)] * reach,
        [HBM] * 3,
        "spectra",
        [
            pltpu.VMEM((blocks, comps, samples, points), BF16),
            pltpu.VMEM(table.shape, BF16),
            pltpu.VMEM((1, points), F32),
            pltpu.VMEM((size, blocks * samples), BF16),
            pltpu.VMEM((groups, *piece), BF16),
            pltpu.SemaphoreType.DMA((steps,)),
            pltpu.SemaphoreType.DMA((2,)),
        ],
    )(in_hbm(snapshots.transpose(0, 2, 1, 3)), table, in_hbm(quad))

    wide, tall = call(
        functools.partial(start_kernel, share, blocks),
        [
            jax.ShapeDtypeStruct((share, size, COPIES * WIDTH), F32),
            jax.ShapeDtypeStruct((share * WIDTH, size), F32),
        ],
        [HBM, pl.BlockSpec(memory_space=pl.ANY)],
        "start",
        [pltpu.VMEM((share, 2, RANK, groups * blocks), F32), pltpu.SemaphoreType.DMA],
    )(in_hbm(omega.transpose(0, 1, 3, 2)), spectra[0])

    arrived = {far: exchange(spectra[far], "blk", 2 * far) for far in range(1, reach)}
    wide, tall, arrived[1] = lax.optimization_barrier((wide, tall, arrived[1]))
    arrived[0] = spectra[0]
    others = {}
    for part in (range(1, reach, 2), range(0, reach, 2)):
        sent = exchange(jnp.stack([arrived[far][1] for far in part]), "blk", 1)
        others |= {far: sent[i] for i, far in enumerate(part)}
    pieces = [piece for far in range(reach) for piece in (arrived[far][0], others[far])]

    packed = (size * (blocks if share * blocks == 8 else height) // height, size)
    gram = call(
        functools.partial(gram_kernel, share, blocks),
        jax.ShapeDtypeStruct(packed, F32),
        [VMEM] * groups,
        "gram",
    )(*pieces)
    if spaces <= 4:
        grams = [gram] + [exchange(gram, "space", d) for d in range(1, spaces)]
    else:
        grams = [lax.psum(gram, "space")]

    coef, energies = call(
        functools.partial(subspace_kernel, share, blocks, width * spaces, len(grams)),
        [
            jax.ShapeDtypeStruct((share * WIDTH, size), BF16),
            jax.ShapeDtypeStruct((NF, RANK), F32),
        ],
        [VMEM] * (len(grams) + 2),
        "subspace",
    )(*grams, wide, tall)

    modes = call(
        functools.partial(modes_kernel, share),
        jax.ShapeDtypeStruct((share, 2, comps, RANK, points), F32),
        [VMEM] * (groups + 2),
        "modes",
    )(quad, coef, *pieces)

    energies = energies + exchange(energies, "blk", 1)
    shares = [exchange(energies, "blk", 2 * far) for far in range(1, reach)]
    for other in shares:
        energies = energies + other
    return modes.transpose(0, 1, 3, 2, 4), energies


def solution(mesh):
    in_specs = (P("blk", None, None, "space"), P("space"), P())
    out_specs = (P("blk", None, None, None, "space"), P())
    return jax.shard_map(
        per_device, mesh=mesh, in_specs=in_specs, out_specs=out_specs, check_vma=False
    )
```
